256 devices in a mesh: grp: 8 (over y, x_hi), seq: 32 (over x_lo, z, core).
Axes of the slice: x: 4 (x_hi: 2, x_lo: 2; x = x_hi * 2 + x_lo), y: 4, z: 8, core: 2. Of those that a mesh axis runs over, the one named last changes fastest.
Arguments:
- gate_in: bfloat16 [32768, 4096], P(('grp', 'seq')), parts along dimension 0, may hold values from -6 to 6
- value_in: bfloat16 [32768, 4096], P(('grp', 'seq')), parts along dimension 0, may hold values from -6 to 6
- gate_out: bfloat16 [32768, 4096], P(('grp', 'seq')), parts along dimension 0, may hold values from -6 to 6
- cotangent: bfloat16 [32768, 4096], P(('grp', 'seq')), parts along dimension 0, may hold values from -3 to 3
- long_filter: float32 [4096, 4096], P(None, 'seq'), may hold values from -1.1 to 1.1
- short_filters: float32 [3, 3, 4096], replicated, may hold values from -3 to 3
Outputs:
- mixed: bfloat16 [32768, 4096], P(('grp', 'seq')), parts along dimension 0
- grad_gate_in: bfloat16 [32768, 4096], P(('grp', 'seq')), parts along dimension 0
- grad_value: bfloat16 [32768, 4096], P(('grp', 'seq')), parts along dimension 0
- grad_gate_out: bfloat16 [32768, 4096], P(('grp', 'seq')), parts along dimension 0
- grad_long: float32 [32768, 4096], P('grp', 'seq'), parts along dimension 0
- grad_short: float32 [24, 3, 4096], P('grp'), parts along dimension 0
The draws below stay inside these ranges and needn't reach their ends.
There are 8 independent parts, one for each index of `grp`. The reference program is written for one: setup_inputs(seed, part) draws one part's arguments, and reference() takes and returns one part's arrays. A program takes and returns all parts, laid end to end along the dimension named above; an argument that names none is the same for every part. Nothing has to cross between parts.
All inputs are finite; a program needn't handle non-finite values.
Results may differ from the reference program's by a relative error of at most 0.02.
Values may be sent and summed in bfloat16 or wider, within the bound.
No kernel may reach another device: no remote copies, remote signals or barrier semaphores. Data moves between devices by JAX's collectives and lax.ppermute only.
A program may use at most 256 MiB of HBM per device.

```python
import jax
import jax.numpy as jnp

D = 4096
TAPS = 3
SEQ = 4096


def draw_long_filter(key, part):
    key = jax.random.fold_in(key, 11)
    rate_key, sample_key = jax.random.split(key)
    log_timescale = jax.random.uniform(rate_key, (1, D), jnp.float32, jnp.log(30.0), jnp.log(4.0 * SEQ))
    sample_draw = jnp.clip(jax.random.normal(sample_key, (SEQ, D), jnp.float32), -4.0, 4.0)
    timescale = jnp.exp(log_timescale)
    positions = jnp.arange(SEQ, dtype=jnp.float32)[:, None]
    norm_factor = jnp.sqrt((1.0 - jnp.exp(-2.0 / timescale)) / (1.0 - jnp.exp(-2.0 * SEQ / timescale)))
    return sample_draw * jnp.exp(-positions / timescale) * norm_factor


def levels(key, dims, cuts, least, top_value):
    gain, own = 1.0, jax.random.fold_in(key, 6)
    for position, blocks in cuts:
        heights = jnp.exp(jax.random.uniform(jax.random.fold_in(own, position), (blocks,), jnp.float32, least / len(cuts), top_value / len(cuts)))
        gain = gain * jnp.repeat(heights, dims[position] // blocks).reshape([-1 if axis == position else 1 for axis in range(len(dims))])
    return gain


def centred(stream_key, dims, scale, reach, pieces=(), kind=jnp.bfloat16):
    array = jax.random.normal(stream_key, dims, jnp.float32) * scale
    if len(pieces) > 0:
        array = levels(stream_key, dims, pieces, -0.22, 0.18) * array
    return jnp.clip(array, min=-reach, max=reach).astype(kind)


def setup_inputs(seed: int = 0, part: int = 0) -> dict:
    streams_of = jax.random.split(jax.random.key(seed), 7)
    part_splits = jax.random.split(jax.random.fold_in(streams_of[6], part), 7)
    return {
        "gate_in": centred(part_splits[0], (SEQ, D), 1.0, 6.0, ((0, 32),)),
        "value_in": centred(part_splits[1], (SEQ, D), 1.0, 6.0, ((0, 32),)),
        "gate_out": centred(part_splits[2], (SEQ, D), 1.0, 6.0, ((0, 32),)),
        "cotangent": centred(part_splits[3], (SEQ, D), 0.5, 3.0, ((0, 32),)),
        "long_filter": draw_long_filter(jax.random.fold_in(streams_of[6], 71), part),
        "short_filters": centred(streams_of[5], (3, TAPS, D), 0.6, 3.0, (), jnp.float32),
    }


def short_causal(extended, taps, count):
    return taps[0] * extended[2:2 + count] + taps[1] * extended[1:1 + count] + taps[2] * extended[0:count]


def short_adjoint(extended, taps, count):
    return taps[0] * extended[0:count] + taps[1] * extended[1:1 + count] + taps[2] * extended[2:2 + count]


def tap_sums(grad_rows, extended, count):
    return jnp.stack([jnp.sum(grad_rows * extended[2 - lag_rows:2 - lag_rows + count], axis=0) for lag_rows in range(3)], axis=0)


def featurize(source, taps, count, width):
    before = jnp.concatenate([jnp.zeros((2, width), jnp.float32), source.astype(jnp.float32)], axis=0)
    return short_causal(before, taps, count).astype(jnp.bfloat16), before


def adjoint_feature(grad_bf, taps, count, width):
    after = jnp.concatenate([grad_bf.astype(jnp.float32), jnp.zeros((2, width), jnp.float32)], axis=0)
    return short_adjoint(after, taps, count).astype(jnp.bfloat16)


def reference(gate_in, value_in, gate_out, cotangent, long_filter, short_filters):
    seq_len = gate_in.shape[0]
    width = gate_in.shape[1]
    fft_len = 2 * seq_len
    feat_gate, ext_gate = featurize(gate_in, short_filters[0], seq_len, width)
    feat_value, ext_value = featurize(value_in, short_filters[1], seq_len, width)
    feat_out, ext_out = featurize(gate_out, short_filters[2], seq_len, width)
    signal = (feat_gate.astype(jnp.float32) * feat_value.astype(jnp.float32)).astype(jnp.bfloat16)
    outer_grad = (feat_out.astype(jnp.float32) * cotangent.astype(jnp.float32)).astype(jnp.bfloat16)
    signal_spec = jnp.fft.rfft(signal.astype(jnp.float32), n=fft_len, axis=0)
    filter_spec = jnp.fft.rfft(long_filter, n=fft_len, axis=0)
    grad_spec = jnp.fft.rfft(outer_grad.astype(jnp.float32), n=fft_len, axis=0)
    conv_out = jnp.fft.irfft(signal_spec * filter_spec, n=fft_len, axis=0)[:seq_len].astype(jnp.bfloat16)
    conv_float = conv_out.astype(jnp.float32)
    mixed = (feat_out.astype(jnp.float32) * conv_float).astype(jnp.bfloat16)
    out_feat_grad = (cotangent.astype(jnp.float32) * conv_float).astype(jnp.bfloat16)
    signal_grad = jnp.fft.irfft(jnp.conj(filter_spec) * grad_spec, n=fft_len, axis=0)[:seq_len].astype(jnp.bfloat16)
    grad_long = jnp.fft.irfft(jnp.conj(signal_spec) * grad_spec, n=fft_len, axis=0)[:seq_len].astype(jnp.float32)
    sig_float = signal_grad.astype(jnp.float32)
    gate_feat_grad = (sig_float * feat_value.astype(jnp.float32)).astype(jnp.bfloat16)
    value_feat_grad = (sig_float * feat_gate.astype(jnp.float32)).astype(jnp.bfloat16)
    grad_gate_in = adjoint_feature(gate_feat_grad, short_filters[0], seq_len, width)
    grad_value = adjoint_feature(value_feat_grad, short_filters[1], seq_len, width)
    grad_gate_out = adjoint_feature(out_feat_grad, short_filters[2], seq_len, width)
    grad_short = jnp.stack([
        tap_sums(gate_feat_grad.astype(jnp.float32), ext_gate, seq_len),
        tap_sums(value_feat_grad.astype(jnp.float32), ext_value, seq_len),
        tap_sums(out_feat_grad.astype(jnp.float32), ext_out, seq_len)], axis=0)
    return (mixed, grad_gate_in, grad_value, grad_gate_out, grad_long, grad_short)
```

```python
import functools

import jax
import jax.numpy as jnp
import ml_dtypes
import numpy as np
from jax import lax
from jax.experimental import pallas as pl
from jax.experimental.pallas import tpu as pltpu
from jax.sharding import PartitionSpec as P

bf16 = jnp.bfloat16
f32 = jnp.float32

TILE = 512
GROUP = 8
PAD = 8


class Sizes:
    def __init__(self, blocks, rows, width):
        self.blocks, self.rows, self.width = blocks, rows, width
        self.half = blocks + 1
        self.parts = -(-2 * self.half // 8) * 8
        self.pitch = rows + PAD
        self.length = 2 * blocks * rows


def tables(z):
    a, b = np.arange(z.half), np.arange(z.blocks)
    turn = 2 * np.pi * ((a[:, None] * b[None, :]) % (2 * z.blocks)) / (2 * z.blocks)
    coarse = np.zeros((z.parts, z.blocks))
    coarse[0 : 2 * z.half : 2] = np.cos(turn)
    coarse[1 : 2 * z.half : 2] = -np.sin(turn)
    weight = np.where((a == 0) | (a == z.blocks), 1.0, 2.0) / z.length
    back = np.zeros((z.blocks, z.parts))
    back[:, 0 : 2 * z.half : 2] = (np.cos(turn) * weight[:, None]).T
    back[:, 1 : 2 * z.half : 2] = (-np.sin(turn) * weight[:, None]).T
    r = np.arange(z.rows)
    phase = ((a[:, None, None] + 2 * z.blocks * r[None, :, None]) * r[None, None, :]) % z.length
    cos_w, sin_w = np.cos(2 * np.pi * phase / z.length), np.sin(2 * np.pi * phase / z.length)
    fine = np.concatenate([np.concatenate([cos_w, sin_w], 2), np.concatenate([-sin_w, cos_w], 2)], 1)
    twice = np.concatenate([coarse, coarse], 1)
    return [t.astype(ml_dtypes.bfloat16) for t in (coarse, twice, fine, fine.transpose(0, 2, 1), back)]


def rows_at(z, block):
    return pl.ds(pl.multiple_of(block * z.pitch, 8), z.rows)


def coarse_forward(z, held, coarse_ref, parts, split):
    coarse = coarse_ref[...]

    def body(step, carry):
        columns = []
        for j in range(GROUP):
            value = held[pl.ds(step * GROUP + j, z.blocks, stride=z.pitch), :]
            high = value.astype(bf16)
            if split:
                high = jnp.concatenate([high, (value - high.astype(f32)).astype(bf16)], axis=0)
            columns.append(high)
        out = jnp.dot(coarse, jnp.concatenate(columns, axis=1), preferred_element_type=f32)
        for j in range(GROUP):
            parts[pl.ds(step * GROUP + j, z.parts, stride=z.pitch), :] = out[:, j * z.width : (j + 1) * z.width]
        return carry

    lax.fori_loop(0, z.rows // GROUP, body, 0)


def coarse_inverse(z, parts, back_ref, held):
    back = back_ref[...]

    def body(step, carry):
        columns = [parts[pl.ds(step * GROUP + j, z.parts, stride=z.pitch), :].astype(bf16) for j in range(GROUP)]
        out = jnp.dot(back, jnp.concatenate(columns, axis=1), preferred_element_type=f32)
        for j in range(GROUP):
            held[pl.ds(step * GROUP + j, z.blocks, stride=z.pitch), :] = out[:, j * z.width : (j + 1) * z.width]
        return carry

    lax.fori_loop(0, z.rows // GROUP, body, 0)


def fine_forward(z, fine_ref, parts, a):
    re = parts[rows_at(z, 2 * a), :].astype(bf16)
    im = parts[rows_at(z, 2 * a + 1), :].astype(bf16)
    return jnp.dot(fine_ref[a], jnp.concatenate([re, im], axis=0), preferred_element_type=f32)


def fine_inverse(z, fine_ref, parts, a, re, im):
    spec = jnp.concatenate([re.astype(bf16), im.astype(bf16)], axis=0)
    out = jnp.dot(fine_ref[a], spec, preferred_element_type=f32)
    parts[rows_at(z, 2 * a), :] = out[: z.rows]
    parts[rows_at(z, 2 * a + 1), :] = out[z.rows :]


def load_blocks(z, block_of, held):
    def body(i, carry):
        held[rows_at(z, i), :] = block_of(i).astype(f32)
        return carry

    lax.fori_loop(0, z.blocks, body, 0, unroll=4)


def filter_kernel(z, filter_ref, twice_ref, fine_ref, spec_ref, held, parts):
    load_blocks(z, lambda i: filter_ref[pl.ds(pl.multiple_of(i * z.rows, 8), z.rows), :], held)
    coarse_forward(z, held, twice_ref, parts, True)

    def body(a, carry):
        spec_ref[a] = fine_forward(z, fine_ref, parts, a).astype(spec_ref.dtype)
        return carry

    lax.fori_loop(0, z.half, body, 0, unroll=3)


def conv_kernel(z, conj, data_ref, filter_ref, coarse_ref, fine_ref, inv_ref, back_ref, spec_ref, out_ref, held, parts):
    load_blocks(z, lambda i: data_ref[i], held)
    coarse_forward(z, held, coarse_ref, parts, False)

    def body(a, carry):
        spec = fine_forward(z, fine_ref, parts, a)
        spec_ref[a] = spec.astype(spec_ref.dtype)
        other = filter_ref[a].astype(f32)
        s_re, s_im, h_re, h_im = spec[: z.rows], spec[z.rows :], other[: z.rows], other[z.rows :]
        if conj:
            re, im = s_re * h_re + s_im * h_im, s_im * h_re - s_re * h_im
        else:
            re, im = s_re * h_re - s_im * h_im, s_re * h_im + s_im * h_re
        fine_inverse(z, inv_ref, parts, a, re, im)
        return carry

    lax.fori_loop(0, z.half, body, 0, unroll=3)
    coarse_inverse(z, parts, back_ref, held)

    def done(i, carry):
        out_ref[i] = held[rows_at(z, i), :].astype(out_ref.dtype)
        return carry

    lax.fori_loop(0, z.blocks, done, 0, unroll=4)


def long_kernel(z, signal_ref, grad_ref, inv_ref, back_ref, out_ref, held, parts):
    spare = (z.parts - 2 * z.half) * z.pitch
    if spare:
        parts[pl.ds(2 * z.half * z.pitch, spare), :] = jnp.zeros((spare, z.width), f32)

    def body(a, carry):
        s, g = signal_ref[a].astype(f32), grad_ref[a].astype(f32)
        s_re, s_im, g_re, g_im = s[: z.rows], s[z.rows :], g[: z.rows], g[z.rows :]
        fine_inverse(z, inv_ref, parts, a, s_re * g_re + s_im * g_im, s_re * g_im - s_im * g_re)
        return carry

    lax.fori_loop(0, z.half, body, 0, unroll=3)
    coarse_inverse(z, parts, back_ref, held)

    def done(i, carry):
        out_ref[pl.ds(pl.multiple_of(i * z.rows, 8), z.rows), :] = held[rows_at(z, i), :]
        return carry

    lax.fori_loop(0, z.blocks, done, 0, unroll=4)


def channel_call(z, kernel, operands, outs, name, cost_us):
    whole = pl.BlockSpec(memory_space=pltpu.VMEM)
    return pl.pallas_call(
        kernel,
        out_shape=outs,
        in_specs=[whole] * len(operands),
        out_specs=[whole] * len(outs),
        scratch_shapes=[
            pltpu.VMEM((z.blocks * z.pitch, z.width), f32),
            pltpu.VMEM((z.parts * z.pitch, z.width), f32),
        ],
        compiler_params=pltpu.CompilerParams(vmem_limit_bytes=40 << 20),
        cost_estimate=pl.CostEstimate(flops=0, bytes_accessed=int(cost_us * 3e6), transcendentals=0),
        name=name,
    )(*operands)


def delayed(rows, before, lag):
    moved = pltpu.roll(rows, lag, 0)
    index = lax.broadcasted_iota(jnp.int32, rows.shape, 0)
    for i in range(lag):
        moved = jnp.where(index == i, before[2 - lag + i : 3 - lag + i], moved)
    return moved


def feature(source, halo, which, taps_ref):
    rows = source.astype(f32)
    before = halo[2 * which : 2 * which + 2]
    one, two = delayed(rows, before, 1), delayed(rows, before, 2)
    taps = taps_ref[which]
    feat = taps[0:1] * rows + taps[1:2] * one + taps[2:3] * two
    return feat.astype(bf16).astype(f32), (rows, one, two)


def outward(out_ref, value):
    for j in range(value.shape[1] // out_ref.shape[2]):
        width = out_ref.shape[2]
        out_ref[j] = value[:, j * width : (j + 1) * width].astype(out_ref.dtype)


def inward(in_ref):
    return jnp.concatenate([in_ref[j] for j in range(in_ref.shape[0])], axis=1).astype(f32)


def outer_kernel(out_ref, cot_ref, halo_ref, taps_ref, outer_ref):
    halo = halo_ref[...].astype(f32)
    feat_out, _ = feature(out_ref[...], halo, 2, taps_ref)
    outward(outer_ref, feat_out * cot_ref[...].astype(f32))


def signal_kernel(gate_ref, value_ref, halo_ref, taps_ref, signal_ref):
    halo = halo_ref[...].astype(f32)
    feat_gate, _ = feature(gate_ref[...], halo, 0, taps_ref)
    feat_value, _ = feature(value_ref[...], halo, 1, taps_ref)
    outward(signal_ref, feat_gate * feat_value)


def adjoint(grad, taps):
    count = grad.shape[0]
    return taps[0:1] * grad + taps[1:2] * pltpu.roll(grad, count - 1, 0) + taps[2:3] * pltpu.roll(grad, count - 2, 0)


def collect(pieces, rows, dtype):
    made = jnp.concatenate(pieces, axis=0)
    spare = rows - made.shape[0]
    if spare:
        made = jnp.concatenate([made, jnp.zeros((spare, made.shape[1]), made.dtype)], axis=0)
    return made.astype(dtype)


def lag_sums(grad, lags):
    return [jnp.sum(grad * lag, axis=0, keepdims=True) for lag in lags]


def input_grads_kernel(
    sig_ref, gate_ref, value_ref, halo_ref, taps_ref, grad_gate_ref, grad_value_ref, sums_ref, head_ref, tail_ref
):
    halo = halo_ref[...].astype(f32)
    sig = inward(sig_ref)
    feat_gate, gate_lags = feature(gate_ref[...], halo, 0, taps_ref)
    feat_value, value_lags = feature(value_ref[...], halo, 1, taps_ref)
    gate_grad = (sig * feat_value).astype(bf16).astype(f32)
    value_grad = (sig * feat_gate).astype(bf16).astype(f32)
    grad_gate_ref[...] = adjoint(gate_grad, taps_ref[0]).astype(bf16)
    grad_value_ref[...] = adjoint(value_grad, taps_ref[1]).astype(bf16)
    sums_ref[...] = collect(lag_sums(gate_grad, gate_lags) + lag_sums(value_grad, value_lags), 8, f32)
    count = sig.shape[0]
    head_ref[...] = collect([gate_grad[0:2], value_grad[0:2]], 8, bf16)
    tail_ref[...] = collect([gate_grad[count - 2 :], value_grad[count - 2 :]], 8, bf16)


def output_grads_kernel(
    conv_ref, out_ref, cot_ref, halo_ref, taps_ref, mixed_ref, grad_out_ref, sums_ref, head_ref, tail_ref
):
    halo = halo_ref[...].astype(f32)
    conv = inward(conv_ref)
    feat_out, out_lags = feature(out_ref[...], halo, 2, taps_ref)
    mixed_ref[...] = (feat_out * conv).astype(bf16)
    out_grad = (cot_ref[...].astype(f32) * conv).astype(bf16).astype(f32)
    grad_out_ref[...] = adjoint(out_grad, taps_ref[2]).astype(bf16)
    sums_ref[...] = collect(lag_sums(out_grad, out_lags), 8, f32)
    count = conv.shape[0]
    head_ref[...] = collect([out_grad[0:2]], 8, bf16)
    tail_ref[...] = collect([out_grad[count - 2 :]], 8, bf16)


def finish_kernel(first, count, *refs):
    ins, head_ref, tail_ref, taps_ref = refs[:count], refs[count], refs[count + 1], refs[count + 2]
    outs = refs[count + 3 :]
    head, tail = head_ref[...].astype(f32), tail_ref[...].astype(f32)
    for k in range(count):
        taps = taps_ref[first + k]
        h0, h1 = head[2 * k : 2 * k + 1], head[2 * k + 1 : 2 * k + 2]
        t0, t1 = tail[2 * k : 2 * k + 1], tail[2 * k + 1 : 2 * k + 2]
        old = ins[k][...].astype(f32)
        index = lax.broadcasted_iota(jnp.int32, old.shape, 0)
        last = old.shape[0] - 1
        new = jnp.where(index == last - 1, taps[0:1] * t0 + taps[1:2] * t1 + taps[2:3] * h0, old)
        new = jnp.where(index == last, taps[0:1] * t1 + taps[1:2] * h0 + taps[2:3] * h1, new)
        outs[k][...] = new.astype(bf16)


def position_call(z, kernel, operands, kinds, out_kinds, channels, name, cost_us, aliases=None):
    tile = TILE if channels % TILE == 0 else z.width

    def spec(kind):
        return {
            "rows": pl.BlockSpec((z.rows, tile), lambda i: (0, i)),
            "moved": pl.BlockSpec((tile // z.width, z.rows, z.width), lambda i: (i, 0, 0)),
            "edge": pl.BlockSpec((8, tile), lambda i: (0, i)),
            "sums": pl.BlockSpec((8, tile), lambda i: (0, i)),
            "taps": pl.BlockSpec((3, 3, tile), lambda i: (0, 0, i)),
            "last": pl.BlockSpec((16, tile), lambda i: (z.rows // 16 - 1, i)),
        }[kind]

    shapes = {
        "rows": jax.ShapeDtypeStruct((z.rows, channels), bf16),
        "last": jax.ShapeDtypeStruct((z.rows, channels), bf16),
        "moved": jax.ShapeDtypeStruct((channels // z.width, z.rows, z.width), bf16),
        "edge": jax.ShapeDtypeStruct((8, channels), bf16),
        "sums": jax.ShapeDtypeStruct((8, channels), f32),
    }
    return pl.pallas_call(
        kernel,
        grid=(channels // tile,),
        out_shape=[shapes[k] for k in out_kinds],
        in_specs=[spec(k) for k in kinds],
        out_specs=[spec(k) for k in out_kinds],
        input_output_aliases=aliases or {},
        compiler_params=pltpu.CompilerParams(vmem_limit_bytes=32 << 20),
        cost_estimate=pl.CostEstimate(flops=0, bytes_accessed=int(cost_us * 3e6), transcendentals=0),
        name=name,
    )(*operands)


def sum_over(value, size):
    bit = 1
    while bit < size:
        value = value + lax.ppermute(value, "seq", [(i, i ^ bit) for i in range(size)])
        bit = 2 * bit
    return value


def exchange(value):
    return lax.all_to_all(value, "seq", split_axis=0, concat_axis=0, tiled=True)


def local(size, gate_in, value_in, gate_out, cotangent, long_filter, short_filters):
    rows, channels = gate_in.shape
    z = Sizes(size, rows, long_filter.shape[1])
    coarse, twice, fine, inv, back = [jnp.asarray(t) for t in tables(z)]
    spec_shape = jax.ShapeDtypeStruct((z.half, 2 * z.rows, z.width), bf16)
    moved_shape = jax.ShapeDtypeStruct((z.blocks, z.rows, z.width), bf16)
    onward = [(i, i + 1) for i in range(size - 1)]
    backward = [(i + 1, i) for i in range(size - 1)]

    edges = jnp.concatenate(
        [gate_in[rows - 2 :], value_in[rows - 2 :], gate_out[rows - 2 :], jnp.zeros((2, channels), bf16)], axis=0
    )
    halo = lax.ppermute(edges, "seq", onward)

    def position(kernel, operands, kinds, outs, name, cost_us, aliases=None):
        return position_call(z, kernel, operands, kinds, outs, channels, name, cost_us, aliases)

    (outer,) = position(
        outer_kernel, (gate_out, cotangent, halo, short_filters), ("rows", "rows", "edge", "taps"), ("moved",), "outer", 4
    )
    (signal,) = position(
        signal_kernel, (gate_in, value_in, halo, short_filters), ("rows", "rows", "edge", "taps"), ("moved",), "signal", 4
    )
    outer_moved = exchange(outer)
    (filter_spec,) = channel_call(
        z, functools.partial(filter_kernel, z), (long_filter, twice, fine), (spec_shape,), "filter_spec", 8
    )
    signal_moved = exchange(signal)
    outer_spec, sig_grad = channel_call(
        z,
        functools.partial(conv_kernel, z, True),
        (outer_moved, filter_spec, coarse, fine, inv, back),
        (spec_shape, moved_shape),
        "signal_grad",
        16,
    )
    sig_rows = exchange(sig_grad)
    signal_spec, conv_out = channel_call(
        z,
        functools.partial(conv_kernel, z, False),
        (signal_moved, filter_spec, coarse, fine, inv, back),
        (spec_shape, moved_shape),
        "conv_out",
        16,
    )
    conv_rows = exchange(conv_out)
    (grad_long,) = channel_call(
        z,
        functools.partial(long_kernel, z),
        (signal_spec, outer_spec, inv, back),
        (jax.ShapeDtypeStruct((z.blocks * z.rows, z.width), f32),),
        "grad_long",
        10,
    )

    grad_gate, grad_value, in_sums, in_head, in_tail = position(
        input_grads_kernel,
        (sig_rows, gate_in, value_in, halo, short_filters),
        ("moved", "rows", "rows", "edge", "taps"),
        ("rows", "rows", "sums", "edge", "edge"),
        "input_grads",
        6,
    )
    in_next = lax.ppermute(in_head, "seq", backward)
    grad_gate, grad_value = position(
        functools.partial(finish_kernel, 0, 2),
        (grad_gate, grad_value, in_next, in_tail, short_filters),
        ("last", "last", "edge", "edge", "taps"),
        ("last", "last"),
        "finish_input_grads",
        2,
        {0: 0, 1: 1},
    )
    in_sums = sum_over(in_sums, size)

    mixed, grad_out, out_sums, out_head, out_tail = position(
        output_grads_kernel,
        (conv_rows, gate_out, cotangent, halo, short_filters),
        ("moved", "rows", "rows", "edge", "taps"),
        ("rows", "rows", "sums", "edge", "edge"),
        "output_grads",
        5,
    )
    out_next = lax.ppermute(out_head, "seq", backward)
    (grad_out,) = position(
        functools.partial(finish_kernel, 2, 1),
        (grad_out, out_next, out_tail, short_filters),
        ("last", "edge", "edge", "taps"),
        ("last",),
        "finish_output_grad",
        2,
        {0: 0},
    )
    out_sums = sum_over(out_sums, size)
    grad_short = jnp.concatenate([in_sums[:6], out_sums[:3]], axis=0).reshape(3, 3, channels)
    return (mixed, grad_gate, grad_value, grad_out, grad_long, grad_short)


def solution(mesh):
    spread = P(("grp", "seq"), None)
    return jax.shard_map(
        functools.partial(local, mesh.shape["seq"]),
        mesh=mesh,
        in_specs=(spread, spread, spread, spread, P(None, "seq"), P()),
        out_specs=(spread, spread, spread, spread, P("grp", "seq"), P("grp", None, None)),
        check_vma=False,
    )
```

```python
import functools

import jax
import jax.numpy as jnp
import ml_dtypes
import numpy as np
from jax import lax
from jax.experimental import pallas as pl
from jax.experimental.pallas import tpu as pltpu
from jax.sharding import PartitionSpec as P

bf16 = jnp.bfloat16
f32 = jnp.float32

TILE = 2048
GROUP = 8
PAD = 8


class Sizes:
    def __init__(self, blocks, rows, width):
        self.blocks, self.rows, self.width = blocks, rows, width
        self.half = blocks + 1
        self.parts = -(-2 * self.half // 8) * 8
        self.pitch = rows + PAD
        self.length = 2 * blocks * rows


def tables(z):
    a, b = np.arange(z.half), np.arange(z.blocks)
    turn = 2 * np.pi * ((a[:, None] * b[None, :]) % (2 * z.blocks)) / (2 * z.blocks)
    coarse = np.zeros((z.parts, z.blocks))
    coarse[0 : 2 * z.half : 2] = np.cos(turn)
    coarse[1 : 2 * z.half : 2] = -np.sin(turn)
    weight = np.where((a == 0) | (a == z.blocks), 1.0, 2.0) / z.length
    back = np.zeros((z.blocks, z.parts))
    back[:, 0 : 2 * z.half : 2] = (np.cos(turn) * weight[:, None]).T
    back[:, 1 : 2 * z.half : 2] = (-np.sin(turn) * weight[:, None]).T
    r = np.arange(z.rows)
    phase = ((a[:, None, None] + 2 * z.blocks * r[None, :, None]) * r[None, None, :]) % z.length
    cos_w, sin_w = np.cos(2 * np.pi * phase / z.length), np.sin(2 * np.pi * phase / z.length)
    fine = np.concatenate([np.concatenate([cos_w, sin_w], 2), np.concatenate([-sin_w, cos_w], 2)], 1)
    twice = np.concatenate([coarse, coarse], 1)
    return [t.astype(ml_dtypes.bfloat16) for t in (coarse, twice, fine, fine.transpose(0, 2, 1), back)]


def rows_at(z, block):
    return pl.ds(pl.multiple_of(block * z.pitch, 8), z.rows)


def coarse_forward(z, held, coarse_ref, parts, split):
    coarse = coarse_ref[...]

    def body(step, carry):
        columns = []
        for j in range(GROUP):
            value = held[pl.ds(step * GROUP + j, z.blocks, stride=z.pitch), :]
            high = value.astype(bf16)
            if split:
                high = jnp.concatenate([high, (value - high.astype(f32)).astype(bf16)], axis=0)
            columns.append(high)
        out = jnp.dot(coarse, jnp.concatenate(columns, axis=1), preferred_element_type=f32)
        for j in range(GROUP):
            parts[pl.ds(step * GROUP + j, z.parts, stride=z.pitch), :] = out[:, j * z.width : (j + 1) * z.width]
        return carry

    lax.fori_loop(0, z.rows // GROUP, body, 0)


def coarse_inverse(z, parts, back_ref, held):
    back = back_ref[...]

    def body(step, carry):
        columns = [parts[pl.ds(step * GROUP + j, z.parts, stride=z.pitch), :].astype(bf16) for j in range(GROUP)]
        out = jnp.dot(back, jnp.concatenate(columns, axis=1), preferred_element_type=f32)
        for j in range(GROUP):
            held[pl.ds(step * GROUP + j, z.blocks, stride=z.pitch), :] = out[:, j * z.width : (j + 1) * z.width]
        return carry

    lax.fori_loop(0, z.rows // GROUP, body, 0)


def fine_forward(z, fine_ref, parts, a):
    re = parts[rows_at(z, 2 * a), :].astype(bf16)
    im = parts[rows_at(z, 2 * a + 1), :].astype(bf16)
    return jnp.dot(fine_ref[a], jnp.concatenate([re, im], axis=0), preferred_element_type=f32)


def fine_inverse(z, fine_ref, targets, a, pairs):
    specs = [jnp.concatenate([re.astype(bf16), im.astype(bf16)], axis=0) for re, im in pairs]
    out = jnp.dot(fine_ref[a], jnp.concatenate(specs, axis=1), preferred_element_type=f32)
    for j, parts in enumerate(targets):
        parts[rows_at(z, 2 * a), :] = out[: z.rows, j * z.width : (j + 1) * z.width]
        parts[rows_at(z, 2 * a + 1), :] = out[z.rows :, j * z.width : (j + 1) * z.width]


def load_blocks(z, block_of, held):
    def body(i, carry):
        held[rows_at(z, i), :] = block_of(i).astype(f32)
        return carry

    lax.fori_loop(0, z.blocks, body, 0, unroll=4)


def store_blocks(z, held, out_ref):
    def body(i, carry):
        out_ref[i] = held[rows_at(z, i), :].astype(out_ref.dtype)
        return carry

    lax.fori_loop(0, z.blocks, body, 0, unroll=4)


def filter_kernel(z, filter_ref, twice_ref, fine_ref, spec_ref, held, parts):
    load_blocks(z, lambda i: filter_ref[pl.ds(pl.multiple_of(i * z.rows, 8), z.rows), :], held)
    coarse_forward(z, held, twice_ref, parts, True)

    def body(a, carry):
        spec_ref[a] = fine_forward(z, fine_ref, parts, a).astype(spec_ref.dtype)
        return carry

    lax.fori_loop(0, z.half, body, 0, unroll=3)


def times(spec, other, rows, conj):
    s_re, s_im, h_re, h_im = spec[:rows], spec[rows:], other[:rows], other[rows:]
    if conj:
        return s_re * h_re + s_im * h_im, s_im * h_re - s_re * h_im
    return s_re * h_re - s_im * h_im, s_re * h_im + s_im * h_re


def signal_grad_kernel(
    z, data_ref, filter_ref, coarse_ref, fine_ref, inv_ref, back_ref, spec_ref, out_ref, held, parts
):
    load_blocks(z, lambda i: data_ref[i], held)
    coarse_forward(z, held, coarse_ref, parts, False)

    def body(a, carry):
        spec = fine_forward(z, fine_ref, parts, a)
        spec_ref[a] = spec.astype(spec_ref.dtype)
        fine_inverse(z, inv_ref, (parts,), a, (times(spec, filter_ref[a].astype(f32), z.rows, True),))
        return carry

    lax.fori_loop(0, z.half, body, 0, unroll=3)
    coarse_inverse(z, parts, back_ref, held)
    store_blocks(z, held, out_ref)


def conv_out_kernel(
    z, data_ref, filter_ref, grad_ref, coarse_ref, fine_ref, inv_ref, back_ref, out_ref, long_ref, held, parts, more
):
    load_blocks(z, lambda i: data_ref[i], held)
    coarse_forward(z, held, coarse_ref, parts, False)
    spare = (z.parts - 2 * z.half) * z.pitch
    if spare:
        more[pl.ds(2 * z.half * z.pitch, spare), :] = jnp.zeros((spare, z.width), f32)

    def body(a, carry):
        spec = fine_forward(z, fine_ref, parts, a)
        conv = times(spec, filter_ref[a].astype(f32), z.rows, False)
        long = times(grad_ref[a].astype(f32), spec, z.rows, True)
        fine_inverse(z, inv_ref, (parts, more), a, (conv, long))
        return carry

    lax.fori_loop(0, z.half, body, 0, unroll=3)
    coarse_inverse(z, parts, back_ref, held)
    store_blocks(z, held, out_ref)
    coarse_inverse(z, more, back_ref, held)

    def done(i, carry):
        long_ref[pl.ds(pl.multiple_of(i * z.rows, 8), z.rows), :] = held[rows_at(z, i), :]
        return carry

    lax.fori_loop(0, z.blocks, done, 0, unroll=4)


def channel_call(z, kernel, operands, outs, name, cost_us, arrays=1):
    whole = pl.BlockSpec(memory_space=pltpu.VMEM)
    return pl.pallas_call(
        kernel,
        out_shape=outs,
        in_specs=[whole] * len(operands),
        out_specs=[whole] * len(outs),
        scratch_shapes=[
            pltpu.VMEM((z.blocks * z.pitch, z.width), f32),
        ]
        + [pltpu.VMEM((z.parts * z.pitch, z.width), f32)] * arrays,
        compiler_params=pltpu.CompilerParams(vmem_limit_bytes=(20 + 8 * arrays) << 20),
        cost_estimate=pl.CostEstimate(flops=0, bytes_accessed=int(cost_us * 3e6), transcendentals=0),
        name=name,
    )(*operands)


def delayed(rows, before, lag):
    moved = pltpu.roll(rows, lag, 0)
    index = lax.broadcasted_iota(jnp.int32, rows.shape, 0)
    for i in range(lag):
        moved = jnp.where(index == i, before[2 - lag + i : 3 - lag + i], moved)
    return moved


def feature(source, halo, which, taps_ref):
    rows = source.astype(f32)
    before = halo[2 * which : 2 * which + 2]
    one, two = delayed(rows, before, 1), delayed(rows, before, 2)
    taps = taps_ref[which]
    feat = taps[0:1] * rows + taps[1:2] * one + taps[2:3] * two
    return feat.astype(bf16).astype(f32), (rows, one, two)


def outward(out_ref, value):
    for j in range(value.shape[1] // out_ref.shape[2]):
        width = out_ref.shape[2]
        out_ref[j] = value[:, j * width : (j + 1) * width].astype(out_ref.dtype)


def inward(in_ref):
    return jnp.concatenate([in_ref[j] for j in range(in_ref.shape[0])], axis=1).astype(f32)


def outer_kernel(out_ref, cot_ref, taps_ref, outer_ref):
    feat_out, _ = feature(out_ref[...], jnp.zeros((8, out_ref.shape[1]), f32), 2, taps_ref)
    outward(outer_ref, feat_out * cot_ref[...].astype(f32))


def outer_head_kernel(old_ref, out_ref, cot_ref, halo_ref, taps_ref, outer_ref):
    feat_out, _ = feature(out_ref[...], halo_ref[...].astype(f32), 2, taps_ref)
    outward(outer_ref, feat_out * cot_ref[...].astype(f32))


def signal_kernel(gate_ref, value_ref, halo_ref, taps_ref, signal_ref):
    halo = halo_ref[...].astype(f32)
    feat_gate, _ = feature(gate_ref[...], halo, 0, taps_ref)
    feat_value, _ = feature(value_ref[...], halo, 1, taps_ref)
    outward(signal_ref, feat_gate * feat_value)


def edges_kernel(gate_ref, value_ref, out_ref, edge_ref):
    rows = [ref[...].astype(f32)[ref.shape[0] - 2 :] for ref in (gate_ref, value_ref, out_ref)]
    edge_ref[...] = collect(rows, 8, bf16)


def adjoint(grad, after, taps):
    index = lax.broadcasted_iota(jnp.int32, grad.shape, 0)
    last = grad.shape[0] - 1
    one = jnp.where(index == last, after[0:1], pltpu.roll(grad, last, 0))
    two = pltpu.roll(grad, last - 1, 0)
    two = jnp.where(index == last - 1, after[0:1], jnp.where(index == last, after[1:2], two))
    return (taps[0:1] * grad + taps[1:2] * one + taps[2:3] * two).astype(bf16)


def collect(pieces, rows, dtype):
    made = jnp.concatenate(pieces, axis=0)
    spare = rows - made.shape[0]
    if spare:
        made = jnp.concatenate([made, jnp.zeros((spare, made.shape[1]), made.dtype)], axis=0)
    return made.astype(dtype)


def lag_sums(grad, lags):
    return [jnp.sum(grad * lag, axis=0, keepdims=True) for lag in lags]


def store_sums(sums_ref, sums):
    made, width = jnp.concatenate(sums, axis=0), sums_ref.shape[2]
    for j in range(sums_ref.shape[0]):
        sums_ref[j] = made[:, j * width : (j + 1) * width]


def input_grads_kernel(
    sig_ref, gate_ref, value_ref, halo_ref, taps_ref, sums_ref, head_ref, tail_ref, grad_gate_ref, grad_value_ref
):
    halo = halo_ref[...].astype(f32)
    sig = inward(sig_ref)
    feat_gate, gate_lags = feature(gate_ref[...], halo, 0, taps_ref)
    feat_value, value_lags = feature(value_ref[...], halo, 1, taps_ref)
    gate_grad = (sig * feat_value).astype(bf16).astype(f32)
    value_grad = (sig * feat_gate).astype(bf16).astype(f32)
    store_sums(sums_ref, lag_sums(gate_grad, gate_lags) + lag_sums(value_grad, value_lags))
    count = sig.shape[0]
    head_ref[...] = collect([gate_grad[0:2], value_grad[0:2]], 8, bf16)
    tail_ref[...] = collect([gate_grad[count - 2 :], value_grad[count - 2 :]], 8, bf16)
    none = jnp.zeros((2, sig.shape[1]), f32)
    grad_gate_ref[...] = adjoint(gate_grad, none, taps_ref[0])
    grad_value_ref[...] = adjoint(value_grad, none, taps_ref[1])


def finish_kernel(gate_ref, value_ref, next_ref, tail_ref, taps_ref, grad_gate_ref, grad_value_ref):
    head, tail = next_ref[...].astype(f32), tail_ref[...].astype(f32)
    for k, (old_ref, new_ref) in enumerate(((gate_ref, grad_gate_ref), (value_ref, grad_value_ref))):
        taps = taps_ref[k]
        t0, t1 = tail[2 * k : 2 * k + 1], tail[2 * k + 1 : 2 * k + 2]
        h0, h1 = head[2 * k : 2 * k + 1], head[2 * k + 1 : 2 * k + 2]
        old = old_ref[...].astype(f32)
        index = lax.broadcasted_iota(jnp.int32, old.shape, 0)
        last = old.shape[0] - 1
        new = jnp.where(index == last - 1, taps[0:1] * t0 + taps[1:2] * t1 + taps[2:3] * h0, old)
        new = jnp.where(index == last, taps[0:1] * t1 + taps[1:2] * h0 + taps[2:3] * h1, new)
        new_ref[...] = new.astype(bf16)


def output_sums_kernel(conv_ref, out_ref, cot_ref, halo_ref, in_head_ref, sums_ref, head_ref):
    before = halo_ref[...].astype(f32)[4:6]
    out_grad = (cot_ref[...].astype(f32) * inward(conv_ref)).astype(bf16).astype(f32)
    rows = out_ref[...].astype(f32)
    lags = (rows, delayed(rows, before, 1), delayed(rows, before, 2))
    store_sums(sums_ref, lag_sums(out_grad, lags))
    head_ref[...] = collect([in_head_ref[...].astype(f32)[0:4], out_grad[0:2]], 8, bf16)


def mixed_kernel(conv_ref, out_ref, halo_ref, taps_ref, mixed_ref):
    feat_out, _ = feature(out_ref[...], halo_ref[...].astype(f32), 2, taps_ref)
    mixed_ref[...] = (feat_out * inward(conv_ref)).astype(bf16)


def output_grad_kernel(conv_ref, cot_ref, next_ref, taps_ref, grad_ref):
    out_grad = (cot_ref[...].astype(f32) * inward(conv_ref)).astype(bf16).astype(f32)
    grad_ref[...] = adjoint(out_grad, next_ref[...].astype(f32)[4:6], taps_ref[2])


def position_call(z, kernel, operands, kinds, out_kinds, channels, name, cost_us, tile=TILE, aliases=None, vmem=14):

    quarter = channels // 4

    def spec(kind):
        return {
            "rows": pl.BlockSpec((z.rows, tile), lambda i: (0, i)),
            "moved": pl.BlockSpec((tile // z.width, z.rows, z.width), lambda i: (i, 0, 0)),
            "edge": pl.BlockSpec((8, tile), lambda i: (0, i)),
            "six": pl.BlockSpec((tile // quarter, 6, quarter), lambda i: (i, 0, 0)),
            "three": pl.BlockSpec((tile // quarter, 3, quarter), lambda i: (i, 0, 0)),
            "taps": pl.BlockSpec((3, 3, tile), lambda i: (0, 0, i)),
            "first": pl.BlockSpec((16, tile), lambda i: (0, i)),
            "moved_first": pl.BlockSpec((tile // z.width, 16, z.width), lambda i: (i, 0, 0)),
            "last": pl.BlockSpec((16, tile), lambda i: (z.rows // 16 - 1, i)),
        }[kind]

    shapes = {
        "rows": jax.ShapeDtypeStruct((z.rows, channels), bf16),
        "last": jax.ShapeDtypeStruct((z.rows, channels), bf16),
        "moved": jax.ShapeDtypeStruct((channels // z.width, z.rows, z.width), bf16),
        "moved_first": jax.ShapeDtypeStruct((channels // z.width, z.rows, z.width), bf16),
        "edge": jax.ShapeDtypeStruct((8, channels), bf16),
        "six": jax.ShapeDtypeStruct((4, 6, quarter), f32),
        "three": jax.ShapeDtypeStruct((4, 3, quarter), f32),
    }
    return pl.pallas_call(
        kernel,
        grid=(channels // tile,),
        out_shape=[shapes[k] for k in out_kinds],
        in_specs=[spec(k) for k in kinds],
        out_specs=[spec(k) for k in out_kinds],
        input_output_aliases=aliases or {},
        compiler_params=pltpu.CompilerParams(vmem_limit_bytes=int(vmem * 2**20)),
        cost_estimate=pl.CostEstimate(flops=0, bytes_accessed=int(cost_us * 3e6), transcendentals=0),
        name=name,
    )(*operands)


class Sums:
    def __init__(self, size):
        self.size, self.depth, self.offsets = size, size // 4, (1, size // 2, size // 2 + 1)
        me = lax.axis_index("seq")
        self.quarter = me % 2 + 2 * (me // (size // 2))

    def swap(self, value, bits):
        return lax.ppermute(value, "seq", [(i, i ^ bits) for i in range(self.size)])

    def piece(self, value, which):
        return lax.dynamic_index_in_dim(value, which, 0, keepdims=False)

    def near(self, value):
        arrived = [self.swap(self.piece(value, self.quarter ^ (k + 1)), bits) for k, bits in enumerate(self.offsets)]
        return (self.piece(value, self.quarter) + arrived[0]) + (arrived[1] + arrived[2])

    def far(self, value):
        lines = [[self.size // 2 * x + 2 * z + core for z in range(self.depth)] for x in range(2) for core in range(2)]
        copies = jnp.broadcast_to(value[None], (self.depth, *value.shape))
        parts = lax.all_to_all(copies, "seq", split_axis=0, concat_axis=0, tiled=True, axis_index_groups=lines)
        return jnp.sum(parts, axis=0)

    def gather(self, value):
        held = jnp.stack([value] + [self.swap(value, bits) for bits in self.offsets])
        return jnp.stack([self.piece(held, self.quarter ^ j) for j in range(4)], axis=1)


def exchange(value):
    return lax.all_to_all(value, "seq", split_axis=0, concat_axis=0, tiled=True)


def local(size, gate_in, value_in, gate_out, cotangent, long_filter, short_filters):
    rows, channels = gate_in.shape
    z = Sizes(size, rows, long_filter.shape[1])
    coarse, twice, fine, inv, back = [jnp.asarray(t) for t in tables(z)]
    spec_shape = jax.ShapeDtypeStruct((z.half, 2 * z.rows, z.width), bf16)
    moved_shape = jax.ShapeDtypeStruct((z.blocks, z.rows, z.width), bf16)
    onward = [(i, i + 1) for i in range(size - 1)]
    backward = [(i + 1, i) for i in range(size - 1)]

    def position(kernel, operands, kinds, outs, name, cost_us, **more):
        return position_call(z, kernel, operands, kinds, outs, channels, name, cost_us, **more)

    (edges,) = position(edges_kernel, (gate_in, value_in, gate_out), ("last",) * 3, ("edge",), "edges", 1, tile=channels, vmem=60)
    halo = lax.ppermute(edges, "seq", onward)

    (outer,) = position(
        outer_kernel,
        (gate_out, cotangent, short_filters),
        ("rows", "rows", "taps"),
        ("moved",),
        "outer",
        4,
        vmem=59.5,
    )
    (outer,) = position(
        outer_head_kernel,
        (outer, gate_out, cotangent, halo, short_filters),
        ("moved_first", "first", "first", "edge", "taps"),
        ("moved_first",),
        "outer_head",
        1,
        tile=channels,
        aliases={0: 0},
        vmem=59.5,
    )
    (signal,) = position(
        signal_kernel, (gate_in, value_in, halo, short_filters), ("rows", "rows", "edge", "taps"), ("moved",), "signal", 4
    )
    outer_moved = exchange(outer)
    (filter_spec,) = channel_call(
        z, functools.partial(filter_kernel, z), (long_filter, twice, fine), (spec_shape,), "filter_spec", 8
    )
    signal, filter_spec = lax.optimization_barrier((signal, filter_spec))
    signal_moved = exchange(signal)
    outer_spec, sig_grad = channel_call(
        z,
        functools.partial(signal_grad_kernel, z),
        (outer_moved, filter_spec, coarse, fine, inv, back),
        (spec_shape, moved_shape),
        "signal_grad",
        16,
    )
    sig_rows = exchange(sig_grad)
    conv_out, grad_long = channel_call(
        z,
        functools.partial(conv_out_kernel, z),
        (signal_moved, filter_spec, outer_spec, coarse, fine, inv, back),
        (moved_shape, jax.ShapeDtypeStruct((z.blocks * z.rows, z.width), f32)),
        "conv_out",
        22,
        arrays=2,
    )
    conv_rows = exchange(conv_out)
    in_sums, in_head, in_tail, grad_gate, grad_value = position(
        input_grads_kernel,
        (sig_rows, gate_in, value_in, halo, short_filters),
        ("moved", "rows", "rows", "edge", "taps"),
        ("six", "edge", "edge", "rows", "rows"),
        "input_grads",
        6,
    )
    sums = Sums(size)
    conv_rows, grad_gate, grad_value, in_sums = lax.optimization_barrier(
        (conv_rows, grad_gate, grad_value, sums.near(in_sums))
    )
    out_sums, out_head = position(
        output_sums_kernel,
        (conv_rows, gate_out, cotangent, halo, in_head),
        ("moved", "rows", "rows", "edge", "edge"),
        ("three", "edge"),
        "output_sums",
        3,
    )
    out_sums, out_head = lax.optimization_barrier((sums.near(out_sums), out_head))
    after = lax.ppermute(out_head, "seq", backward)
    (mixed,) = position(
        mixed_kernel,
        (conv_rows, gate_out, halo, short_filters),
        ("moved", "rows", "edge", "taps"),
        ("rows",),
        "mixed",
        3,
    )
    both = jnp.concatenate([in_sums, out_sums], axis=0).reshape(9, -1, z.width)
    (grad_out,) = position(
        output_grad_kernel,
        (conv_rows, cotangent, after, short_filters),
        ("moved", "rows", "edge", "taps"),
        ("rows",),
        "output_grad",
        3,
    )
    both, grad_out = lax.optimization_barrier((sums.far(both), grad_out))
    grad_gate, grad_value = position(
        finish_kernel,
        (grad_gate, grad_value, after, in_tail, short_filters),
        ("last", "last", "edge", "edge", "taps"),
        ("last", "last"),
        "finish_input_grads",
        2,
        tile=channels,
        aliases={0: 0, 1: 1},
    )
    grad_short = sums.gather(both).reshape(3, 3, channels)
    return (mixed, grad_gate, grad_value, grad_out, grad_long, grad_short)


def solution(mesh):
    spread = P(("grp", "seq"), None)
    return jax.shard_map(
        functools.partial(local, mesh.shape["seq"]),
        mesh=mesh,
        in_specs=(spread, spread, spread, spread, P(None, "seq"), P()),
        out_specs=(spread, spread, spread, spread, P("grp", "seq"), P("grp", None, None)),
        check_vma=False,
    )
```

```python
import functools

import jax
import jax.numpy as jnp
import ml_dtypes
import numpy as np
from jax import lax
from jax.experimental import pallas as pl
from jax.experimental.pallas import tpu as pltpu
from jax.sharding import PartitionSpec as P

bf16 = jnp.bfloat16
f32 = jnp.float32

TILE = 2048
GROUP = 32
PAD = 8


class Sizes:
    def __init__(self, blocks, rows, width):
        self.blocks, self.rows, self.width = blocks, rows, width
        self.half = blocks + 1
        self.parts = -(-2 * self.half // 8) * 8
        self.pitch = rows + PAD
        self.length = 2 * blocks * rows
        self.halves = blocks // 16
        self.pack = -(-18 * self.halves // 8) * 8


def tables(z):
    a, b = np.arange(z.half), np.arange(z.blocks)
    turn = 2 * np.pi * ((a[:, None] * b[None, :]) % (2 * z.blocks)) / (2 * z.blocks)
    coarse = np.zeros((z.parts, z.blocks))
    coarse[0 : 2 * z.half : 2] = np.cos(turn)
    coarse[1 : 2 * z.half : 2] = -np.sin(turn)
    weight = np.where((a == 0) | (a == z.blocks), 1.0, 2.0) / z.length
    back = np.zeros((z.blocks, z.parts))
    back[:, 0 : 2 * z.half : 2] = (np.cos(turn) * weight[:, None]).T
    back[:, 1 : 2 * z.half : 2] = (-np.sin(turn) * weight[:, None]).T
    r = np.arange(z.rows)
    phase = ((a[:, None, None] + 2 * z.blocks * r[None, :, None]) * r[None, None, :]) % z.length
    cos_w, sin_w = np.cos(2 * np.pi * phase / z.length), np.sin(2 * np.pi * phase / z.length)
    fine = np.concatenate([np.concatenate([cos_w, sin_w], 2), np.concatenate([-sin_w, cos_w], 2)], 1)
    twice = np.concatenate([coarse, coarse], 1)
    return [t.astype(ml_dtypes.bfloat16) for t in (coarse, twice, fine, fine.transpose(0, 2, 1), back)]


def rows_at(z, block):
    return pl.ds(pl.multiple_of(block * z.pitch, 8), z.rows)


def coarse_forward(z, held, coarse_ref, parts, split):
    coarse = coarse_ref[...]

    def body(step, carry):
        columns = []
        for j in range(GROUP):
            value = held[pl.ds(step * GROUP + j, z.blocks, stride=z.pitch), :]
            high = value.astype(bf16)
            if split:
                high = jnp.concatenate([high, (value - high.astype(f32)).astype(bf16)], axis=0)
            columns.append(high)
        out = jnp.dot(coarse, jnp.concatenate(columns, axis=1), preferred_element_type=f32)
        for j in range(GROUP):
            parts[pl.ds(step * GROUP + j, z.parts, stride=z.pitch), :] = out[:, j * z.width : (j + 1) * z.width]
        return carry

    lax.fori_loop(0, z.rows // GROUP, body, 0)


def coarse_inverse(z, parts, back_ref, held):
    back = back_ref[...]

    def body(step, carry):
        columns = [parts[pl.ds(step * GROUP + j, z.parts, stride=z.pitch), :].astype(bf16) for j in range(GROUP)]
        out = jnp.dot(back, jnp.concatenate(columns, axis=1), preferred_element_type=f32)
        for j in range(GROUP):
            held[pl.ds(step * GROUP + j, z.blocks, stride=z.pitch), :] = out[:, j * z.width : (j + 1) * z.width]
        return carry

    lax.fori_loop(0, z.rows // GROUP, body, 0)


def fine_forward(z, fine_ref, parts, a):
    re = parts[rows_at(z, 2 * a), :].astype(bf16)
    im = parts[rows_at(z, 2 * a + 1), :].astype(bf16)
    return jnp.dot(fine_ref[a], jnp.concatenate([re, im], axis=0), preferred_element_type=f32)


def fine_inverse(z, fine_ref, targets, a, pairs):
    specs = [jnp.concatenate([re.astype(bf16), im.astype(bf16)], axis=0) for re, im in pairs]
    out = jnp.dot(fine_ref[a], jnp.concatenate(specs, axis=1), preferred_element_type=f32)
    for j, parts in enumerate(targets):
        parts[rows_at(z, 2 * a), :] = out[: z.rows, j * z.width : (j + 1) * z.width]
        parts[rows_at(z, 2 * a + 1), :] = out[z.rows :, j * z.width : (j + 1) * z.width]


def load_blocks(z, block_of, held):
    def body(i, carry):
        held[rows_at(z, i), :] = block_of(i).astype(f32)
        return carry

    lax.fori_loop(0, z.blocks, body, 0, unroll=4)


def store_blocks(z, held, out_ref):
    def body(i, carry):
        out_ref[i] = held[rows_at(z, i), :].astype(out_ref.dtype)
        return carry

    lax.fori_loop(0, z.blocks, body, 0, unroll=4)


def filter_kernel(z, filter_ref, twice_ref, fine_ref, spec_ref, held, parts):
    load_blocks(z, lambda i: filter_ref[pl.ds(pl.multiple_of(i * z.rows, 8), z.rows), :], held)
    coarse_forward(z, held, twice_ref, parts, True)

    def body(a, carry):
        spec_ref[a] = fine_forward(z, fine_ref, parts, a).astype(spec_ref.dtype)
        return carry

    lax.fori_loop(0, z.half, body, 0, unroll=11)


def times(spec, other, rows, conj):
    s_re, s_im, h_re, h_im = spec[:rows], spec[rows:], other[:rows], other[rows:]
    if conj:
        return s_re * h_re + s_im * h_im, s_im * h_re - s_re * h_im
    return s_re * h_re - s_im * h_im, s_re * h_im + s_im * h_re


def signal_grad_kernel(
    z, data_ref, filter_ref, coarse_ref, fine_ref, inv_ref, back_ref, spec_ref, out_ref, held, parts
):
    load_blocks(z, lambda i: data_ref[i], held)
    coarse_forward(z, held, coarse_ref, parts, False)

    def body(a, carry):
        spec = fine_forward(z, fine_ref, parts, a)
        spec_ref[a] = spec.astype(spec_ref.dtype)
        fine_inverse(z, inv_ref, (parts,), a, (times(spec, filter_ref[a].astype(f32), z.rows, True),))
        return carry

    lax.fori_loop(0, z.half, body, 0, unroll=11)
    coarse_inverse(z, parts, back_ref, held)
    store_blocks(z, held, out_ref)


def conv_out_kernel(
    z, data_ref, filter_ref, grad_ref, coarse_ref, fine_ref, inv_ref, back_ref, out_ref, long_ref, held, parts, more
):
    load_blocks(z, lambda i: data_ref[i], held)
    coarse_forward(z, held, coarse_ref, parts, False)
    spare = (z.parts - 2 * z.half) * z.pitch
    if spare:
        more[pl.ds(2 * z.half * z.pitch, spare), :] = jnp.zeros((spare, z.width), f32)

    def body(a, carry):
        spec = fine_forward(z, fine_ref, parts, a)
        conv = times(spec, filter_ref[a].astype(f32), z.rows, False)
        long = times(grad_ref[a].astype(f32), spec, z.rows, True)
        fine_inverse(z, inv_ref, (parts, more), a, (conv, long))
        return carry

    lax.fori_loop(0, z.half, body, 0, unroll=11)
    coarse_inverse(z, parts, back_ref, held)
    store_blocks(z, held, out_ref)
    coarse_inverse(z, more, back_ref, held)

    def done(i, carry):
        long_ref[pl.ds(pl.multiple_of(i * z.rows, 8), z.rows), :] = held[rows_at(z, i), :]
        return carry

    lax.fori_loop(0, z.blocks, done, 0, unroll=4)


def channel_call(z, kernel, operands, outs, name, cost_us, arrays=1):
    whole = pl.BlockSpec(memory_space=pltpu.VMEM)
    return pl.pallas_call(
        kernel,
        out_shape=outs,
        in_specs=[whole] * len(operands),
        out_specs=[whole] * len(outs),
        scratch_shapes=[
            pltpu.VMEM((z.blocks * z.pitch, z.width), f32),
        ]
        + [pltpu.VMEM((z.parts * z.pitch, z.width), f32)] * arrays,
        compiler_params=pltpu.CompilerParams(vmem_limit_bytes=(20 + 8 * arrays) << 20),
        cost_estimate=pl.CostEstimate(flops=0, bytes_accessed=int(cost_us * 3e6), transcendentals=0),
        name=name,
    )(*operands)


def delayed(rows, before, lag):
    moved = pltpu.roll(rows, lag, 0)
    index = lax.broadcasted_iota(jnp.int32, rows.shape, 0)
    for i in range(lag):
        moved = jnp.where(index == i, before[2 - lag + i : 3 - lag + i], moved)
    return moved


def feature(source, halo, which, taps_ref):
    rows = source.astype(f32)
    before = halo[2 * which : 2 * which + 2]
    one, two = delayed(rows, before, 1), delayed(rows, before, 2)
    taps = taps_ref[which]
    feat = taps[0:1] * rows + taps[1:2] * one + taps[2:3] * two
    return feat.astype(bf16).astype(f32), (rows, one, two)


def outward(out_ref, value):
    for j in range(value.shape[1] // out_ref.shape[2]):
        width = out_ref.shape[2]
        out_ref[j] = value[:, j * width : (j + 1) * width].astype(out_ref.dtype)


def inward(in_ref):
    return jnp.concatenate([in_ref[j] for j in range(in_ref.shape[0])], axis=1).astype(f32)


def outer_kernel(out_ref, cot_ref, taps_ref, outer_ref):
    feat_out, _ = feature(out_ref[...], jnp.zeros((8, out_ref.shape[1]), f32), 2, taps_ref)
    outward(outer_ref, feat_out * cot_ref[...].astype(f32))


def outer_head_kernel(old_ref, out_ref, cot_ref, halo_ref, taps_ref, outer_ref):
    feat_out, _ = feature(out_ref[...], halo_ref[...].astype(f32), 2, taps_ref)
    outward(outer_ref, feat_out * cot_ref[...].astype(f32))


def signal_kernel(gate_ref, value_ref, halo_ref, taps_ref, signal_ref):
    halo = halo_ref[...].astype(f32)
    feat_gate, _ = feature(gate_ref[...], halo, 0, taps_ref)
    feat_value, _ = feature(value_ref[...], halo, 1, taps_ref)
    outward(signal_ref, feat_gate * feat_value)


def edges_kernel(gate_ref, value_ref, out_ref, edge_ref):
    rows = [ref[...].astype(f32)[ref.shape[0] - 2 :] for ref in (gate_ref, value_ref, out_ref)]
    edge_ref[...] = collect(rows, 8, bf16)


def adjoint(grad, after, taps):
    index = lax.broadcasted_iota(jnp.int32, grad.shape, 0)
    last = grad.shape[0] - 1
    one = jnp.where(index == last, after[0:1], pltpu.roll(grad, last, 0))
    two = pltpu.roll(grad, last - 1, 0)
    two = jnp.where(index == last - 1, after[0:1], jnp.where(index == last, after[1:2], two))
    return (taps[0:1] * grad + taps[1:2] * one + taps[2:3] * two).astype(bf16)


def collect(pieces, rows, dtype):
    made = jnp.concatenate(pieces, axis=0)
    spare = rows - made.shape[0]
    if spare:
        made = jnp.concatenate([made, jnp.zeros((spare, made.shape[1]), made.dtype)], axis=0)
    return made.astype(dtype)


def lag_sums(grad, lags):
    return [jnp.sum(grad * lag, axis=0, keepdims=True) for lag in lags]


def store_sums(sums_ref, sums):
    made, width = jnp.concatenate(sums, axis=0), sums_ref.shape[2]
    for j in range(sums_ref.shape[0]):
        sums_ref[j] = made[:, j * width : (j + 1) * width]


def input_grads_kernel(
    sig_ref, gate_ref, value_ref, halo_ref, taps_ref, sums_ref, head_ref, tail_ref, grad_gate_ref, grad_value_ref
):
    halo = halo_ref[...].astype(f32)
    sig = inward(sig_ref)
    feat_gate, gate_lags = feature(gate_ref[...], halo, 0, taps_ref)
    feat_value, value_lags = feature(value_ref[...], halo, 1, taps_ref)
    gate_grad = (sig * feat_value).astype(bf16).astype(f32)
    value_grad = (sig * feat_gate).astype(bf16).astype(f32)
    store_sums(sums_ref, lag_sums(gate_grad, gate_lags) + lag_sums(value_grad, value_lags))
    count = sig.shape[0]
    head_ref[...] = collect([gate_grad[0:2], value_grad[0:2]], 8, bf16)
    tail_ref[...] = collect([gate_grad[count - 2 :], value_grad[count - 2 :]], 8, bf16)
    none = jnp.zeros((2, sig.shape[1]), f32)
    grad_gate_ref[...] = adjoint(gate_grad, none, taps_ref[0])
    grad_value_ref[...] = adjoint(value_grad, none, taps_ref[1])


def finish_kernel(gate_ref, value_ref, next_ref, tail_ref, taps_ref, grad_gate_ref, grad_value_ref):
    head, tail = next_ref[...].astype(f32), tail_ref[...].astype(f32)
    for k, (old_ref, new_ref) in enumerate(((gate_ref, grad_gate_ref), (value_ref, grad_value_ref))):
        taps = taps_ref[k]
        t0, t1 = tail[2 * k : 2 * k + 1], tail[2 * k + 1 : 2 * k + 2]
        h0, h1 = head[2 * k : 2 * k + 1], head[2 * k + 1 : 2 * k + 2]
        old = old_ref[...].astype(f32)
        index = lax.broadcasted_iota(jnp.int32, old.shape, 0)
        last = old.shape[0] - 1
        new = jnp.where(index == last - 1, taps[0:1] * t0 + taps[1:2] * t1 + taps[2:3] * h0, old)
        new = jnp.where(index == last, taps[0:1] * t1 + taps[1:2] * h0 + taps[2:3] * h1, new)
        new_ref[...] = new.astype(bf16)


def output_sums_kernel(conv_ref, out_ref, cot_ref, halo_ref, in_sums_ref, packet_ref, head_ref):
    before = halo_ref[...].astype(f32)[4:6]
    out_grad = (cot_ref[...].astype(f32) * inward(conv_ref)).astype(bf16).astype(f32)
    rows = out_ref[...].astype(f32)
    lags = (rows, delayed(rows, before, 1), delayed(rows, before, 2))
    sums, ins = jnp.concatenate(lag_sums(out_grad, lags), axis=0), in_sums_ref[...]
    head_ref[...] = collect([out_grad[0:2]], 8, bf16)
    count, pack, width = packet_ref.shape
    quarter = sums.shape[1] // 4
    part = quarter // 4
    for n in range(4):
        pieces = [
            sums[:, q * quarter + n * part + h : q * quarter + n * part + h + width]
            for q in range(4)
            for h in range(0, part, width)
        ]
        pieces += [ins[:, n * part + h : n * part + h + width] for h in range(0, part, width)]
        packet = collect(pieces, pack, bf16)
        for depth in range(count // 4):
            packet_ref[(n // 2) * (count // 2) + 2 * depth + n % 2] = packet


def packet_sums_kernel(packet_ref, total_ref):
    count, _, width = packet_ref.shape
    halves = total_ref.shape[0] // 36
    outs = 12 * halves
    packets = [packet_ref[d].astype(f32) for d in range(count)]
    near = [
        functools.reduce(jnp.add, [packets[(q // 2) * (count // 2) + 2 * depth + q % 2] for depth in range(count // 4)])
        for q in range(4)
    ]
    whole = (near[0] + near[1]) + (near[2] + near[3])
    pieces = [whole[:outs]] + [part[outs : outs + 6 * halves] for part in near]
    total_ref[...] = jnp.concatenate(pieces, axis=0)


def short_kernel(me_ref, held_ref, short_ref):
    quarter = short_ref.shape[2] // 4
    part, width = quarter // 4, held_ref.shape[2]
    halves = part // width
    for n in range(4):
        held = held_ref[me_ref[0] ^ n]
        for q in range(4):
            for h in range(halves):
                start = q * quarter + n * part + h * width
                out_row = (q * halves + h) * 3
                in_row = 12 * halves + (q * halves + h) * 6
                short_ref[0, :, start : start + width] = held[in_row : in_row + 3]
                short_ref[1, :, start : start + width] = held[in_row + 3 : in_row + 6]
                short_ref[2, :, start : start + width] = held[out_row : out_row + 3]


def mixed_kernel(conv_ref, out_ref, halo_ref, taps_ref, mixed_ref):
    feat_out, _ = feature(out_ref[...], halo_ref[...].astype(f32), 2, taps_ref)
    mixed_ref[...] = (feat_out * inward(conv_ref)).astype(bf16)


def output_grad_kernel(conv_ref, cot_ref, next_ref, taps_ref, grad_ref):
    out_grad = (cot_ref[...].astype(f32) * inward(conv_ref)).astype(bf16).astype(f32)
    grad_ref[...] = adjoint(out_grad, next_ref[...].astype(f32)[0:2], taps_ref[2])


def position_call(z, kernel, operands, kinds, out_kinds, channels, name, cost_us, tile=TILE, aliases=None, vmem=14):

    quarter = channels // 4

    def spec(kind):
        return {
            "rows": pl.BlockSpec((z.rows, tile), lambda i: (0, i)),
            "moved": pl.BlockSpec((tile // z.width, z.rows, z.width), lambda i: (i, 0, 0)),
            "edge": pl.BlockSpec((8, tile), lambda i: (0, i)),
            "six": pl.BlockSpec((tile // quarter, 6, quarter), lambda i: (i, 0, 0)),
            "near": pl.BlockSpec((6, quarter), lambda i: (0, 0)),
            "taps": pl.BlockSpec((3, 3, tile), lambda i: (0, 0, i)),
            "left": pl.BlockSpec(memory_space=pl.ANY),
            "whole": pl.BlockSpec(memory_space=pltpu.VMEM),
            "packet": pl.BlockSpec((z.blocks, z.pack, z.width), lambda i: (0, 0, 0)),
            "first": pl.BlockSpec((16, tile), lambda i: (0, i)),
            "moved_first": pl.BlockSpec((tile // z.width, 16, z.width), lambda i: (i, 0, 0)),
            "last": pl.BlockSpec((16, tile), lambda i: (z.rows // 16 - 1, i)),
        }[kind]

    shapes = {
        "rows": jax.ShapeDtypeStruct((z.rows, channels), bf16),
        "last": jax.ShapeDtypeStruct((z.rows, channels), bf16),
        "moved": jax.ShapeDtypeStruct((channels // z.width, z.rows, z.width), bf16),
        "moved_first": jax.ShapeDtypeStruct((channels // z.width, z.rows, z.width), bf16),
        "packet": jax.ShapeDtypeStruct((z.blocks, z.pack, z.width), bf16),
        "edge": jax.ShapeDtypeStruct((8, channels), bf16),
        "six": jax.ShapeDtypeStruct((4, 6, quarter), f32),
    }
    return pl.pallas_call(
        kernel,
        grid=(channels // tile,),
        out_shape=[shapes[k] for k in out_kinds],
        in_specs=[spec(k) for k in kinds],
        out_specs=[spec(k) for k in out_kinds],
        input_output_aliases=aliases or {},
        compiler_params=pltpu.CompilerParams(vmem_limit_bytes=int(vmem * 2**20)),
        cost_estimate=pl.CostEstimate(flops=0, bytes_accessed=int(cost_us * 3e6), transcendentals=0),
        name=name,
    )(*operands)


def small_call(kernel, operands, out, name, scalars=0):
    spaces = [pltpu.SMEM] * scalars + [pltpu.VMEM] * (len(operands) - scalars)
    return pl.pallas_call(
        kernel,
        out_shape=[out],
        in_specs=[pl.BlockSpec(memory_space=space) for space in spaces],
        out_specs=[pl.BlockSpec(memory_space=pltpu.VMEM)],
        compiler_params=pltpu.CompilerParams(vmem_limit_bytes=8 << 20),
        cost_estimate=pl.CostEstimate(flops=0, bytes_accessed=3000000, transcendentals=0),
        name=name,
    )(*operands)


class Near:
    def __init__(self, size):
        self.size, self.offsets = size, (1, size // 2, size // 2 + 1)
        me = lax.axis_index("seq")
        self.quarter = me % 2 + 2 * (me // (size // 2))

    def swap(self, value, bits):
        return lax.ppermute(value, "seq", [(i, i ^ bits) for i in range(self.size)])

    def piece(self, value, which):
        return lax.dynamic_index_in_dim(value, which, 0, keepdims=False)

    def scatter(self, value):
        arrived = [self.swap(self.piece(value, self.quarter ^ (k + 1)), bits) for k, bits in enumerate(self.offsets)]
        return (self.piece(value, self.quarter) + arrived[0]) + (arrived[1] + arrived[2])

    def gather(self, value):
        return jnp.stack([value] + [self.swap(value, bits) for bits in self.offsets])


def exchange(value):
    return lax.all_to_all(value, "seq", split_axis=0, concat_axis=0, tiled=True)


def local(size, gate_in, value_in, gate_out, cotangent, long_filter, short_filters):
    rows, channels = gate_in.shape
    z = Sizes(size, rows, long_filter.shape[1])
    coarse, twice, fine, inv, back = [jnp.asarray(t) for t in tables(z)]
    spec_shape = jax.ShapeDtypeStruct((z.half, 2 * z.rows, z.width), bf16)
    moved_shape = jax.ShapeDtypeStruct((z.blocks, z.rows, z.width), bf16)
    onward = [(i, i + 1) for i in range(size - 1)]
    backward = [(i + 1, i) for i in range(size - 1)]

    def position(kernel, operands, kinds, outs, name, cost_us, **more):
        return position_call(z, kernel, operands, kinds, outs, channels, name, cost_us, **more)

    (edges,) = position(edges_kernel, (gate_in, value_in, gate_out), ("last",) * 3, ("edge",), "edges", 1, tile=channels, vmem=60)
    halo = lax.ppermute(edges, "seq", onward)

    (outer,) = position(
        outer_kernel,
        (gate_out, cotangent, short_filters),
        ("rows", "rows", "taps"),
        ("moved",),
        "outer",
        4,
        vmem=59.5,
    )
    (outer,) = position(
        outer_head_kernel,
        (outer, gate_out, cotangent, halo, short_filters),
        ("left", "first", "first", "whole", "taps"),
        ("moved_first",),
        "outer_head",
        1,
        tile=channels,
        aliases={0: 0},
        vmem=59.5,
    )
    (signal,) = position(
        signal_kernel, (gate_in, value_in, halo, short_filters), ("rows", "rows", "edge", "taps"), ("moved",), "signal", 4
    )
    outer_moved = exchange(outer)
    (filter_spec,) = channel_call(
        z, functools.partial(filter_kernel, z), (long_filter, twice, fine), (spec_shape,), "filter_spec", 8
    )
    signal, filter_spec = lax.optimization_barrier((signal, filter_spec))
    signal_moved = exchange(signal)
    outer_spec, sig_grad = channel_call(
        z,
        functools.partial(signal_grad_kernel, z),
        (outer_moved, filter_spec, coarse, fine, inv, back),
        (spec_shape, moved_shape),
        "signal_grad",
        16,
    )
    sig_rows = exchange(sig_grad)
    conv_out, grad_long = channel_call(
        z,
        functools.partial(conv_out_kernel, z),
        (signal_moved, filter_spec, outer_spec, coarse, fine, inv, back),
        (moved_shape, jax.ShapeDtypeStruct((z.blocks * z.rows, z.width), f32)),
        "conv_out",
        22,
        arrays=2,
    )
    conv_rows = exchange(conv_out)
    in_sums, in_head, in_tail, grad_gate, grad_value = position(
        input_grads_kernel,
        (sig_rows, gate_in, value_in, halo, short_filters),
        ("moved", "rows", "rows", "edge", "taps"),
        ("six", "edge", "edge", "rows", "rows"),
        "input_grads",
        6,
    )
    near = Near(size)
    in_sums = near.scatter(in_sums)
    in_after = lax.ppermute(in_head, "seq", backward)
    packets, out_head = position(
        output_sums_kernel,
        (conv_rows, gate_out, cotangent, halo, in_sums),
        ("moved", "rows", "rows", "edge", "near"),
        ("packet", "edge"),
        "output_sums",
        3,
        tile=channels,
    )
    after = lax.ppermute(out_head, "seq", backward)
    packets = exchange(packets)
    (mixed,) = position(
        mixed_kernel,
        (conv_rows, gate_out, halo, short_filters),
        ("moved", "rows", "edge", "taps"),
        ("rows",),
        "mixed",
        3,
    )
    (grad_out,) = position(
        output_grad_kernel,
        (conv_rows, cotangent, after, short_filters),
        ("moved", "rows", "edge", "taps"),
        ("rows",),
        "output_grad",
        3,
    )
    grad_gate, grad_value = position(
        finish_kernel,
        (grad_gate, grad_value, in_after, in_tail, short_filters),
        ("last", "last", "edge", "edge", "taps"),
        ("last", "last"),
        "finish_input_grads",
        2,
        tile=channels,
        aliases={0: 0, 1: 1},
    )
    packets, mixed, grad_out, grad_gate, grad_value = lax.optimization_barrier(
        (packets, mixed, grad_out, grad_gate, grad_value)
    )
    (total,) = small_call(
        packet_sums_kernel, (packets,), jax.ShapeDtypeStruct((36 * z.halves, z.width), f32), "packet_sums"
    )
    held = near.gather(total)
    quarter = near.quarter.astype(jnp.int32).reshape(1)
    (grad_short,) = small_call(
        short_kernel, (quarter, held), jax.ShapeDtypeStruct((3, 3, channels), f32), "grad_short", scalars=1
    )
    return (mixed, grad_gate, grad_value, grad_out, grad_long, grad_short)


def solution(mesh):
    spread = P(("grp", "seq"), None)
    return jax.shard_map(
        functools.partial(local, mesh.shape["seq"]),
        mesh=mesh,
        in_specs=(spread, spread, spread, spread, P(None, "seq"), P()),
        out_specs=(spread, spread, spread, spread, P("grp", "seq"), P("grp", None, None)),
        check_vma=False,
    )
```

```python
import functools

import jax
import jax.numpy as jnp
import ml_dtypes
import numpy as np
from jax import lax
from jax.experimental import pallas as pl
from jax.experimental.pallas import tpu as pltpu
from jax.sharding import PartitionSpec as P

bf16 = jnp.bfloat16
f32 = jnp.float32

TILE = 2048
GROUP = 32
PAD = 8


class Sizes:
    def __init__(self, blocks, rows, width):
        self.blocks, self.rows, self.width = blocks, rows, width
        self.half = blocks + 1
        self.parts = -(-2 * self.half // 8) * 8
        self.pitch = rows + PAD
        self.length = 2 * blocks * rows
        self.halves = blocks // 16
        self.pack = -(-18 * self.halves // 8) * 8


def tables(z):
    a, b = np.arange(z.half), np.arange(z.blocks)
    turn = 2 * np.pi * ((a[:, None] * b[None, :]) % (2 * z.blocks)) / (2 * z.blocks)
    coarse = np.zeros((z.parts, z.blocks))
    coarse[0 : 2 * z.half : 2] = np.cos(turn)
    coarse[1 : 2 * z.half : 2] = -np.sin(turn)
    weight = np.where((a == 0) | (a == z.blocks), 1.0, 2.0) / z.length
    back = np.zeros((z.blocks, z.parts))
    back[:, 0 : 2 * z.half : 2] = (np.cos(turn) * weight[:, None]).T
    back[:, 1 : 2 * z.half : 2] = (-np.sin(turn) * weight[:, None]).T
    r = np.arange(z.rows)
    phase = ((a[:, None, None] + 2 * z.blocks * r[None, :, None]) * r[None, None, :]) % z.length
    cos_w, sin_w = np.cos(2 * np.pi * phase / z.length), np.sin(2 * np.pi * phase / z.length)
    fine = np.concatenate([np.concatenate([cos_w, sin_w], 2), np.concatenate([-sin_w, cos_w], 2)], 1)
    twice = np.concatenate([coarse, coarse], 1)
    return [t.astype(ml_dtypes.bfloat16) for t in (coarse, twice, fine, fine.transpose(0, 2, 1), back)]


def rows_at(z, block):
    return pl.ds(pl.multiple_of(block * z.pitch, 8), z.rows)


def coarse_forward(z, held, coarse_ref, parts, split):
    coarse = coarse_ref[...]

    def body(step, carry):
        columns = []
        for j in range(GROUP):
            value = held[pl.ds(step * GROUP + j, z.blocks, stride=z.pitch), :]
            high = value.astype(bf16)
            if split:
                high = jnp.concatenate([high, (value - high.astype(f32)).astype(bf16)], axis=0)
            columns.append(high)
        out = jnp.dot(coarse, jnp.concatenate(columns, axis=1), preferred_element_type=f32)
        for j in range(GROUP):
            parts[pl.ds(step * GROUP + j, z.parts, stride=z.pitch), :] = out[:, j * z.width : (j + 1) * z.width]
        return carry

    lax.fori_loop(0, z.rows // GROUP, body, 0)


def coarse_inverse(z, parts, back_ref, held):
    back = back_ref[...]

    def body(step, carry):
        columns = [parts[pl.ds(step * GROUP + j, z.parts, stride=z.pitch), :].astype(bf16) for j in range(GROUP)]
        out = jnp.dot(back, jnp.concatenate(columns, axis=1), preferred_element_type=f32)
        for j in range(GROUP):
            held[pl.ds(step * GROUP + j, z.blocks, stride=z.pitch), :] = out[:, j * z.width : (j + 1) * z.width]
        return carry

    lax.fori_loop(0, z.rows // GROUP, body, 0)


def fine_forward(z, fine_ref, parts, a):
    re = parts[rows_at(z, 2 * a), :].astype(bf16)
    im = parts[rows_at(z, 2 * a + 1), :].astype(bf16)
    return jnp.dot(fine_ref[a], jnp.concatenate([re, im], axis=0), preferred_element_type=f32)


def fine_inverse(z, fine_ref, targets, a, pairs):
    specs = [jnp.concatenate([re.astype(bf16), im.astype(bf16)], axis=0) for re, im in pairs]
    out = jnp.dot(fine_ref[a], jnp.concatenate(specs, axis=1), preferred_element_type=f32)
    for j, parts in enumerate(targets):
        parts[rows_at(z, 2 * a), :] = out[: z.rows, j * z.width : (j + 1) * z.width]
        parts[rows_at(z, 2 * a + 1), :] = out[z.rows :, j * z.width : (j + 1) * z.width]


def load_blocks(z, block_of, held):
    def body(i, carry):
        held[rows_at(z, i), :] = block_of(i).astype(f32)
        return carry

    lax.fori_loop(0, z.blocks, body, 0, unroll=4)


def store_blocks(z, held, out_ref):
    def body(i, carry):
        out_ref[i] = held[rows_at(z, i), :].astype(out_ref.dtype)
        return carry

    lax.fori_loop(0, z.blocks, body, 0, unroll=4)


def filter_kernel(z, filter_ref, twice_ref, fine_ref, spec_ref, held, parts):
    load_blocks(z, lambda i: filter_ref[pl.ds(pl.multiple_of(i * z.rows, 8), z.rows), :], held)
    coarse_forward(z, held, twice_ref, parts, True)

    def body(a, carry):
        spec_ref[a] = fine_forward(z, fine_ref, parts, a).astype(spec_ref.dtype)
        return carry

    lax.fori_loop(0, z.half, body, 0, unroll=11)


def times(spec, other, rows, conj):
    s_re, s_im, h_re, h_im = spec[:rows], spec[rows:], other[:rows], other[rows:]
    if conj:
        return s_re * h_re + s_im * h_im, s_im * h_re - s_re * h_im
    return s_re * h_re - s_im * h_im, s_re * h_im + s_im * h_re


def load_longer(z, data_ref, held):
    def body(i, carry):
        held[pl.ds(pl.multiple_of(i * z.pitch, 8), z.pitch), :] = data_ref[i].astype(f32)
        return carry

    lax.fori_loop(0, z.blocks, body, 0, unroll=4)


def spare_rows(z, held, start, count):
    return [held[pl.ds(z.rows + start + k, z.blocks, stride=z.pitch), :] for k in range(count)]


def first_features(z, held, start, taps):
    last, end, first, second = spare_rows(z, held, start, 4)
    top = lax.broadcasted_iota(jnp.int32, last.shape, 0) == 0
    two_before, before = [jnp.where(top, 0.0, pltpu.roll(rows, 1, 0)) for rows in (last, end)]
    return [
        (taps[0:1] * now + taps[1:2] * one + taps[2:3] * two).astype(bf16).astype(f32)
        for now, one, two in ((first, before, two_before), (second, first, before))
    ]


def put_first_rows(z, held, products):
    for k, (left, right) in enumerate(products):
        held[pl.ds(k, z.blocks, stride=z.pitch), :] = (left * right).astype(bf16).astype(f32)


def signal_grad_kernel(
    z, data_ref, taps_ref, filter_ref, coarse_ref, fine_ref, inv_ref, back_ref, spec_ref, out_ref, held, parts
):
    load_longer(z, data_ref, held)
    put_first_rows(z, held, zip(first_features(z, held, 0, taps_ref[2]), spare_rows(z, held, 4, 2)))
    coarse_forward(z, held, coarse_ref, parts, False)

    def body(a, carry):
        spec = fine_forward(z, fine_ref, parts, a)
        spec_ref[a] = spec.astype(spec_ref.dtype)
        fine_inverse(z, inv_ref, (parts,), a, (times(spec, filter_ref[a].astype(f32), z.rows, True),))
        return carry

    lax.fori_loop(0, z.half, body, 0, unroll=11)
    coarse_inverse(z, parts, back_ref, held)
    store_blocks(z, held, out_ref)


def conv_out_kernel(
    z,
    data_ref,
    taps_ref,
    filter_ref,
    grad_ref,
    coarse_ref,
    fine_ref,
    inv_ref,
    back_ref,
    out_ref,
    long_ref,
    held,
    parts,
    more,
):
    load_longer(z, data_ref, held)
    put_first_rows(
        z, held, zip(first_features(z, held, 0, taps_ref[0]), first_features(z, held, 4, taps_ref[1]))
    )
    coarse_forward(z, held, coarse_ref, parts, False)
    spare = (z.parts - 2 * z.half) * z.pitch
    if spare:
        more[pl.ds(2 * z.half * z.pitch, spare), :] = jnp.zeros((spare, z.width), f32)

    def body(a, carry):
        spec = fine_forward(z, fine_ref, parts, a)
        conv = times(spec, filter_ref[a].astype(f32), z.rows, False)
        long = times(grad_ref[a].astype(f32), spec, z.rows, True)
        fine_inverse(z, inv_ref, (parts, more), a, (conv, long))
        return carry

    lax.fori_loop(0, z.half, body, 0, unroll=11)
    coarse_inverse(z, parts, back_ref, held)
    store_blocks(z, held, out_ref)
    coarse_inverse(z, more, back_ref, held)

    def done(i, carry):
        long_ref[pl.ds(pl.multiple_of(i * z.rows, 8), z.rows), :] = held[rows_at(z, i), :]
        return carry

    lax.fori_loop(0, z.blocks, done, 0, unroll=4)


def channel_call(z, kernel, operands, outs, name, cost_us, arrays=1):
    whole = pl.BlockSpec(memory_space=pltpu.VMEM)
    return pl.pallas_call(
        kernel,
        out_shape=outs,
        in_specs=[whole] * len(operands),
        out_specs=[whole] * len(outs),
        scratch_shapes=[
            pltpu.VMEM((z.blocks * z.pitch, z.width), f32),
        ]
        + [pltpu.VMEM((z.parts * z.pitch, z.width), f32)] * arrays,
        compiler_params=pltpu.CompilerParams(vmem_limit_bytes=(20 + 8 * arrays) << 20),
        cost_estimate=pl.CostEstimate(flops=0, bytes_accessed=int(cost_us * 3e6), transcendentals=0),
        name=name,
    )(*operands)


def delayed(rows, before, lag):
    moved = pltpu.roll(rows, lag, 0)
    index = lax.broadcasted_iota(jnp.int32, rows.shape, 0)
    for i in range(lag):
        moved = jnp.where(index == i, before[2 - lag + i : 3 - lag + i], moved)
    return moved


def feature(source, halo, which, taps_ref):
    rows = source.astype(f32)
    before = halo[2 * which : 2 * which + 2]
    one, two = delayed(rows, before, 1), delayed(rows, before, 2)
    taps = taps_ref[which]
    feat = taps[0:1] * rows + taps[1:2] * one + taps[2:3] * two
    return feat.astype(bf16).astype(f32), (rows, one, two)


def outward(out_ref, value):
    for j in range(value.shape[1] // out_ref.shape[2]):
        width = out_ref.shape[2]
        out_ref[j] = value[:, j * width : (j + 1) * width].astype(out_ref.dtype)


def inward(in_ref):
    return jnp.concatenate([in_ref[j] for j in range(in_ref.shape[0])], axis=1).astype(f32)


def outer_kernel(out_ref, cot_ref, taps_ref, outer_ref):
    rows, cot = out_ref[...].astype(f32), cot_ref[...].astype(f32)
    feat_out, _ = feature(out_ref[...], jnp.zeros((8, rows.shape[1]), f32), 2, taps_ref)
    more = collect([rows[rows.shape[0] - 2 :], rows[0:2], cot[0:2]], PAD, f32)
    outward(outer_ref, jnp.concatenate([feat_out * cot, more], axis=0))


def signal_kernel(gate_ref, value_ref, taps_ref, signal_ref):
    none = jnp.zeros((8, gate_ref.shape[1]), f32)
    feat_gate, (gate, _, _) = feature(gate_ref[...], none, 0, taps_ref)
    feat_value, (value, _, _) = feature(value_ref[...], none, 1, taps_ref)
    count = gate.shape[0]
    more = collect([gate[count - 2 :], gate[0:2], value[count - 2 :], value[0:2]], PAD, f32)
    outward(signal_ref, jnp.concatenate([feat_gate * feat_value, more], axis=0))


def edges_kernel(gate_ref, value_ref, out_ref, edge_ref):
    rows = [ref[...].astype(f32)[ref.shape[0] - 2 :] for ref in (gate_ref, value_ref, out_ref)]
    edge_ref[...] = collect(rows, 8, bf16)


def adjoint(grad, after, taps):
    index = lax.broadcasted_iota(jnp.int32, grad.shape, 0)
    last = grad.shape[0] - 1
    one = jnp.where(index == last, after[0:1], pltpu.roll(grad, last, 0))
    two = pltpu.roll(grad, last - 1, 0)
    two = jnp.where(index == last - 1, after[0:1], jnp.where(index == last, after[1:2], two))
    return (taps[0:1] * grad + taps[1:2] * one + taps[2:3] * two).astype(bf16)


def collect(pieces, rows, dtype):
    made = jnp.concatenate(pieces, axis=0)
    spare = rows - made.shape[0]
    if spare:
        made = jnp.concatenate([made, jnp.zeros((spare, made.shape[1]), made.dtype)], axis=0)
    return made.astype(dtype)


def lag_sums(grad, lags):
    return [jnp.sum(grad * lag, axis=0, keepdims=True) for lag in lags]


def store_sums(sums_ref, sums):
    made, width = jnp.concatenate(sums, axis=0), sums_ref.shape[2]
    for j in range(sums_ref.shape[0]):
        sums_ref[j] = made[:, j * width : (j + 1) * width]


def input_grads_kernel(
    sig_ref, gate_ref, value_ref, halo_ref, taps_ref, sums_ref, head_ref, tail_ref, grad_gate_ref, grad_value_ref
):
    halo = halo_ref[...].astype(f32)
    sig = inward(sig_ref)
    feat_gate, gate_lags = feature(gate_ref[...], halo, 0, taps_ref)
    feat_value, value_lags = feature(value_ref[...], halo, 1, taps_ref)
    gate_grad = (sig * feat_value).astype(bf16).astype(f32)
    value_grad = (sig * feat_gate).astype(bf16).astype(f32)
    store_sums(sums_ref, lag_sums(gate_grad, gate_lags) + lag_sums(value_grad, value_lags))
    count = sig.shape[0]
    head_ref[...] = collect([gate_grad[0:2], value_grad[0:2]], 8, bf16)
    tail_ref[...] = collect([gate_grad[count - 2 :], value_grad[count - 2 :]], 8, bf16)
    none = jnp.zeros((2, sig.shape[1]), f32)
    grad_gate_ref[...] = adjoint(gate_grad, none, taps_ref[0])
    grad_value_ref[...] = adjoint(value_grad, none, taps_ref[1])


def finish_kernel(gate_ref, value_ref, next_ref, tail_ref, taps_ref, grad_gate_ref, grad_value_ref):
    head, tail = next_ref[...].astype(f32), tail_ref[...].astype(f32)
    for k, (old_ref, new_ref) in enumerate(((gate_ref, grad_gate_ref), (value_ref, grad_value_ref))):
        taps = taps_ref[k]
        t0, t1 = tail[2 * k : 2 * k + 1], tail[2 * k + 1 : 2 * k + 2]
        h0, h1 = head[2 * k : 2 * k + 1], head[2 * k + 1 : 2 * k + 2]
        old = old_ref[...].astype(f32)
        index = lax.broadcasted_iota(jnp.int32, old.shape, 0)
        last = old.shape[0] - 1
        new = jnp.where(index == last - 1, taps[0:1] * t0 + taps[1:2] * t1 + taps[2:3] * h0, old)
        new = jnp.where(index == last, taps[0:1] * t1 + taps[1:2] * h0 + taps[2:3] * h1, new)
        new_ref[...] = new.astype(bf16)


def output_sums_kernel(conv_ref, out_ref, cot_ref, halo_ref, in_sums_ref, packet_ref, head_ref):
    before = halo_ref[...].astype(f32)[4:6]
    out_grad = (cot_ref[...].astype(f32) * inward(conv_ref)).astype(bf16).astype(f32)
    rows = out_ref[...].astype(f32)
    lags = (rows, delayed(rows, before, 1), delayed(rows, before, 2))
    sums, ins = jnp.concatenate(lag_sums(out_grad, lags), axis=0), in_sums_ref[...]
    head_ref[...] = collect([out_grad[0:2]], 8, bf16)
    count, pack, width = packet_ref.shape
    quarter = sums.shape[1] // 4
    part = quarter // 4
    for n in range(4):
        pieces = [
            sums[:, q * quarter + n * part + h : q * quarter + n * part + h + width]
            for q in range(4)
            for h in range(0, part, width)
        ]
        pieces += [ins[:, n * part + h : n * part + h + width] for h in range(0, part, width)]
        packet = collect(pieces, pack, bf16)
        for depth in range(count // 4):
            packet_ref[(n // 2) * (count // 2) + 2 * depth + n % 2] = packet


def packet_sums_kernel(packet_ref, total_ref):
    count, _, width = packet_ref.shape
    halves = total_ref.shape[0] // 36
    outs = 12 * halves
    packets = [packet_ref[d].astype(f32) for d in range(count)]
    near = [
        functools.reduce(jnp.add, [packets[(q // 2) * (count // 2) + 2 * depth + q % 2] for depth in range(count // 4)])
        for q in range(4)
    ]
    whole = (near[0] + near[1]) + (near[2] + near[3])
    pieces = [whole[:outs]] + [part[outs : outs + 6 * halves] for part in near]
    total_ref[...] = jnp.concatenate(pieces, axis=0)


def short_kernel(me_ref, held_ref, short_ref):
    quarter = short_ref.shape[2] // 4
    part, width = quarter // 4, held_ref.shape[2]
    halves = part // width
    for n in range(4):
        held = held_ref[me_ref[0] ^ n]
        for q in range(4):
            for h in range(halves):
                start = q * quarter + n * part + h * width
                out_row = (q * halves + h) * 3
                in_row = 12 * halves + (q * halves + h) * 6
                short_ref[0, :, start : start + width] = held[in_row : in_row + 3]
                short_ref[1, :, start : start + width] = held[in_row + 3 : in_row + 6]
                short_ref[2, :, start : start + width] = held[out_row : out_row + 3]


def mixed_kernel(conv_ref, out_ref, halo_ref, taps_ref, mixed_ref):
    feat_out, _ = feature(out_ref[...], halo_ref[...].astype(f32), 2, taps_ref)
    mixed_ref[...] = (feat_out * inward(conv_ref)).astype(bf16)


def output_grad_kernel(conv_ref, cot_ref, next_ref, taps_ref, grad_ref):
    out_grad = (cot_ref[...].astype(f32) * inward(conv_ref)).astype(bf16).astype(f32)
    grad_ref[...] = adjoint(out_grad, next_ref[...].astype(f32)[0:2], taps_ref[2])


def position_call(z, kernel, operands, kinds, out_kinds, channels, name, cost_us, tile=TILE, aliases=None, vmem=14):

    quarter = channels // 4

    def spec(kind):
        return {
            "rows": pl.BlockSpec((z.rows, tile), lambda i: (0, i)),
            "moved": pl.BlockSpec((tile // z.width, z.rows, z.width), lambda i: (i, 0, 0)),
            "edge": pl.BlockSpec((8, tile), lambda i: (0, i)),
            "six": pl.BlockSpec((tile // quarter, 6, quarter), lambda i: (i, 0, 0)),
            "near": pl.BlockSpec((6, quarter), lambda i: (0, 0)),
            "taps": pl.BlockSpec((3, 3, tile), lambda i: (0, 0, i)),
            "packet": pl.BlockSpec((z.blocks, z.pack, z.width), lambda i: (0, 0, 0)),
            "longer": pl.BlockSpec((tile // z.width, z.pitch, z.width), lambda i: (i, 0, 0)),
            "last": pl.BlockSpec((16, tile), lambda i: (z.rows // 16 - 1, i)),
        }[kind]

    shapes = {
        "rows": jax.ShapeDtypeStruct((z.rows, channels), bf16),
        "last": jax.ShapeDtypeStruct((z.rows, channels), bf16),
        "moved": jax.ShapeDtypeStruct((channels // z.width, z.rows, z.width), bf16),
        "longer": jax.ShapeDtypeStruct((channels // z.width, z.pitch, z.width), bf16),
        "packet": jax.ShapeDtypeStruct((z.blocks, z.pack, z.width), bf16),
        "edge": jax.ShapeDtypeStruct((8, channels), bf16),
        "six": jax.ShapeDtypeStruct((4, 6, quarter), f32),
    }
    return pl.pallas_call(
        kernel,
        grid=(channels // tile,),
        out_shape=[shapes[k] for k in out_kinds],
        in_specs=[spec(k) for k in kinds],
        out_specs=[spec(k) for k in out_kinds],
        input_output_aliases=aliases or {},
        compiler_params=pltpu.CompilerParams(vmem_limit_bytes=int(vmem * 2**20)),
        cost_estimate=pl.CostEstimate(flops=0, bytes_accessed=int(cost_us * 3e6), transcendentals=0),
        name=name,
    )(*operands)


def small_call(kernel, operands, out, name, scalars=0):
    spaces = [pltpu.SMEM] * scalars + [pltpu.VMEM] * (len(operands) - scalars)
    return pl.pallas_call(
        kernel,
        out_shape=[out],
        in_specs=[pl.BlockSpec(memory_space=space) for space in spaces],
        out_specs=[pl.BlockSpec(memory_space=pltpu.VMEM)],
        compiler_params=pltpu.CompilerParams(vmem_limit_bytes=8 << 20),
        cost_estimate=pl.CostEstimate(flops=0, bytes_accessed=3000000, transcendentals=0),
        name=name,
    )(*operands)


class Near:
    def __init__(self, size):
        self.size, self.offsets = size, (1, size // 2, size // 2 + 1)
        me = lax.axis_index("seq")
        self.quarter = me % 2 + 2 * (me // (size // 2))

    def swap(self, value, bits):
        return lax.ppermute(value, "seq", [(i, i ^ bits) for i in range(self.size)])

    def piece(self, value, which):
        return lax.dynamic_index_in_dim(value, which, 0, keepdims=False)

    def scatter(self, value):
        arrived = [self.swap(self.piece(value, self.quarter ^ (k + 1)), bits) for k, bits in enumerate(self.offsets)]
        return (self.piece(value, self.quarter) + arrived[0]) + (arrived[1] + arrived[2])

    def gather(self, value):
        return jnp.stack([value] + [self.swap(value, bits) for bits in self.offsets])


def exchange(value):
    return lax.all_to_all(value, "seq", split_axis=0, concat_axis=0, tiled=True)


def local(size, gate_in, value_in, gate_out, cotangent, long_filter, short_filters):
    rows, channels = gate_in.shape
    z = Sizes(size, rows, long_filter.shape[1])
    coarse, twice, fine, inv, back = [jnp.asarray(t) for t in tables(z)]
    spec_shape = jax.ShapeDtypeStruct((z.half, 2 * z.rows, z.width), bf16)
    moved_shape = jax.ShapeDtypeStruct((z.blocks, z.rows, z.width), bf16)
    onward = [(i, i + 1) for i in range(size - 1)]
    backward = [(i + 1, i) for i in range(size - 1)]

    def position(kernel, operands, kinds, outs, name, cost_us, **more):
        return position_call(z, kernel, operands, kinds, outs, channels, name, cost_us, **more)

    (outer,) = position(
        outer_kernel,
        (gate_out, cotangent, short_filters),
        ("rows", "rows", "taps"),
        ("longer",),
        "outer",
        4,
        vmem=60,
    )
    outer, last_gate = lax.optimization_barrier((outer, gate_in))
    (edges,) = position(
        edges_kernel, (last_gate, value_in, gate_out), ("last",) * 3, ("edge",), "edges", 1, tile=channels
    )
    halo = lax.ppermute(edges, "seq", onward)
    (signal,) = position(
        signal_kernel, (gate_in, value_in, short_filters), ("rows", "rows", "taps"), ("longer",), "signal", 4
    )
    outer_moved = exchange(outer)
    taps_here = lax.dynamic_slice_in_dim(short_filters, lax.axis_index("seq") * z.width, z.width, 2)
    (filter_spec,) = channel_call(
        z, functools.partial(filter_kernel, z), (long_filter, twice, fine), (spec_shape,), "filter_spec", 8
    )
    signal, filter_spec, halo = lax.optimization_barrier((signal, filter_spec, halo))
    signal_moved = exchange(signal)
    outer_spec, sig_grad = channel_call(
        z,
        functools.partial(signal_grad_kernel, z),
        (outer_moved, taps_here, filter_spec, coarse, fine, inv, back),
        (spec_shape, moved_shape),
        "signal_grad",
        16,
    )
    sig_rows = exchange(sig_grad)
    conv_out, grad_long = channel_call(
        z,
        functools.partial(conv_out_kernel, z),
        (signal_moved, taps_here, filter_spec, outer_spec, coarse, fine, inv, back),
        (moved_shape, jax.ShapeDtypeStruct((z.blocks * z.rows, z.width), f32)),
        "conv_out",
        22,
        arrays=2,
    )
    conv_rows = exchange(conv_out)
    in_sums, in_head, in_tail, grad_gate, grad_value = position(
        input_grads_kernel,
        (sig_rows, gate_in, value_in, halo, short_filters),
        ("moved", "rows", "rows", "edge", "taps"),
        ("six", "edge", "edge", "rows", "rows"),
        "input_grads",
        6,
    )
    near = Near(size)
    in_sums = near.scatter(in_sums)
    in_after = lax.ppermute(in_head, "seq", backward)
    packets, out_head = position(
        output_sums_kernel,
        (conv_rows, gate_out, cotangent, halo, in_sums),
        ("moved", "rows", "rows", "edge", "near"),
        ("packet", "edge"),
        "output_sums",
        3,
        tile=channels,
    )
    after = lax.ppermute(out_head, "seq", backward)
    packets = exchange(packets)
    (mixed,) = position(
        mixed_kernel,
        (conv_rows, gate_out, halo, short_filters),
        ("moved", "rows", "edge", "taps"),
        ("rows",),
        "mixed",
        3,
    )
    (grad_out,) = position(
        output_grad_kernel,
        (conv_rows, cotangent, after, short_filters),
        ("moved", "rows", "edge", "taps"),
        ("rows",),
        "output_grad",
        3,
    )
    grad_gate, grad_value = position(
        finish_kernel,
        (grad_gate, grad_value, in_after, in_tail, short_filters),
        ("last", "last", "edge", "edge", "taps"),
        ("last", "last"),
        "finish_input_grads",
        2,
        tile=channels,
        aliases={0: 0, 1: 1},
    )
    packets, mixed, grad_out, grad_gate, grad_value = lax.optimization_barrier(
        (packets, mixed, grad_out, grad_gate, grad_value)
    )
    (total,) = small_call(
        packet_sums_kernel, (packets,), jax.ShapeDtypeStruct((36 * z.halves, z.width), f32), "packet_sums"
    )
    held = near.gather(total)
    quarter = near.quarter.astype(jnp.int32).reshape(1)
    (grad_short,) = small_call(
        short_kernel, (quarter, held), jax.ShapeDtypeStruct((3, 3, channels), f32), "grad_short", scalars=1
    )
    return (mixed, grad_gate, grad_value, grad_out, grad_long, grad_short)


def solution(mesh):
    spread = P(("grp", "seq"), None)
    return jax.shard_map(
        functools.partial(local, mesh.shape["seq"]),
        mesh=mesh,
        in_specs=(spread, spread, spread, spread, P(None, "seq"), P()),
        out_specs=(spread, spread, spread, spread, P("grp", "seq"), P("grp", None, None)),
        check_vma=False,
    )
```

```python
import functools

import jax
import jax.numpy as jnp
import ml_dtypes
import numpy as np
from jax import lax
from jax.experimental import pallas as pl
from jax.experimental.pallas import tpu as pltpu
from jax.sharding import PartitionSpec as P

bf16 = jnp.bfloat16
f32 = jnp.float32

TILE = 2048
GROUP = 32
PAD = 8


class Sizes:
    def __init__(self, blocks, rows, width):
        self.blocks, self.rows, self.width = blocks, rows, width
        self.half = blocks + 1
        self.parts = -(-2 * self.half // 8) * 8
        self.pitch = rows + PAD
        self.length = 2 * blocks * rows
        self.halves = blocks // 16
        self.pack = -(-18 * self.halves // 8) * 8


def tables(z):
    a, b = np.arange(z.half), np.arange(z.blocks)
    turn = 2 * np.pi * ((a[:, None] * b[None, :]) % (2 * z.blocks)) / (2 * z.blocks)
    coarse = np.zeros((z.parts, z.blocks))
    coarse[0 : 2 * z.half : 2] = np.cos(turn)
    coarse[1 : 2 * z.half : 2] = -np.sin(turn)
    weight = np.where((a == 0) | (a == z.blocks), 1.0, 2.0) / z.length
    back = np.zeros((z.blocks, z.parts))
    back[:, 0 : 2 * z.half : 2] = (np.cos(turn) * weight[:, None]).T
    back[:, 1 : 2 * z.half : 2] = (-np.sin(turn) * weight[:, None]).T
    r = np.arange(z.rows)
    phase = ((a[:, None, None] + 2 * z.blocks * r[None, :, None]) * r[None, None, :]) % z.length
    cos_w, sin_w = np.cos(2 * np.pi * phase / z.length), np.sin(2 * np.pi * phase / z.length)
    fine = np.concatenate([np.concatenate([cos_w, sin_w], 2), np.concatenate([-sin_w, cos_w], 2)], 1)
    twice = np.concatenate([coarse, coarse], 1)
    return [t.astype(ml_dtypes.bfloat16) for t in (coarse, twice, fine, fine.transpose(0, 2, 1), back)]


def rows_at(z, block):
    return pl.ds(pl.multiple_of(block * z.pitch, 8), z.rows)


def coarse_forward(z, held, coarse_ref, parts, split):
    coarse = coarse_ref[...]

    def body(step, carry):
        columns = []
        for j in range(GROUP):
            value = held[pl.ds(step * GROUP + j, z.blocks, stride=z.pitch), :]
            high = value.astype(bf16)
            if split:
                high = jnp.concatenate([high, (value - high.astype(f32)).astype(bf16)], axis=0)
            columns.append(high)
        out = jnp.dot(coarse, jnp.concatenate(columns, axis=1), preferred_element_type=f32)
        for j in range(GROUP):
            parts[pl.ds(step * GROUP + j, z.parts, stride=z.pitch), :] = out[:, j * z.width : (j + 1) * z.width]
        return carry

    lax.fori_loop(0, z.rows // GROUP, body, 0)


def coarse_inverse(z, parts, back_ref, held):
    back = back_ref[...]

    def body(step, carry):
        columns = [parts[pl.ds(step * GROUP + j, z.parts, stride=z.pitch), :].astype(bf16) for j in range(GROUP)]
        out = jnp.dot(back, jnp.concatenate(columns, axis=1), preferred_element_type=f32)
        for j in range(GROUP):
            held[pl.ds(step * GROUP + j, z.blocks, stride=z.pitch), :] = out[:, j * z.width : (j + 1) * z.width]
        return carry

    lax.fori_loop(0, z.rows // GROUP, body, 0)


def fine_forward(z, fine_ref, parts, a):
    re = parts[rows_at(z, 2 * a), :].astype(bf16)
    im = parts[rows_at(z, 2 * a + 1), :].astype(bf16)
    return jnp.dot(fine_ref[a], jnp.concatenate([re, im], axis=0), preferred_element_type=f32)


def fine_inverse(z, fine_ref, targets, a, pairs):
    specs = [jnp.concatenate([re.astype(bf16), im.astype(bf16)], axis=0) for re, im in pairs]
    out = jnp.dot(fine_ref[a], jnp.concatenate(specs, axis=1), preferred_element_type=f32)
    for j, parts in enumerate(targets):
        parts[rows_at(z, 2 * a), :] = out[: z.rows, j * z.width : (j + 1) * z.width]
        parts[rows_at(z, 2 * a + 1), :] = out[z.rows :, j * z.width : (j + 1) * z.width]


def load_blocks(z, block_of, held):
    def body(i, carry):
        held[rows_at(z, i), :] = block_of(i).astype(f32)
        return carry

    lax.fori_loop(0, z.blocks, body, 0, unroll=4)


def store_blocks(z, held, out_ref):
    def body(i, carry):
        out_ref[i] = held[rows_at(z, i), :].astype(out_ref.dtype)
        return carry

    lax.fori_loop(0, z.blocks, body, 0, unroll=4)


def filter_kernel(z, filter_ref, twice_ref, fine_ref, spec_ref, held, parts):
    load_blocks(z, lambda i: filter_ref[pl.ds(pl.multiple_of(i * z.rows, 8), z.rows), :], held)
    coarse_forward(z, held, twice_ref, parts, True)

    def body(a, carry):
        spec_ref[a] = fine_forward(z, fine_ref, parts, a).astype(spec_ref.dtype)
        return carry

    lax.fori_loop(0, z.half, body, 0, unroll=11)


def times(spec, other, rows, conj):
    s_re, s_im, h_re, h_im = spec[:rows], spec[rows:], other[:rows], other[rows:]
    if conj:
        return s_re * h_re + s_im * h_im, s_im * h_re - s_re * h_im
    return s_re * h_re - s_im * h_im, s_re * h_im + s_im * h_re


def load_longer(z, data_ref, held):
    def body(i, carry):
        held[pl.ds(pl.multiple_of(i * z.pitch, 8), z.pitch), :] = data_ref[i].astype(f32)
        return carry

    lax.fori_loop(0, z.blocks, body, 0, unroll=4)


def spare_rows(z, held, start, count):
    return [held[pl.ds(z.rows + start + k, z.blocks, stride=z.pitch), :] for k in range(count)]


def first_features(z, held, start, taps):
    last, end, first, second = spare_rows(z, held, start, 4)
    top = lax.broadcasted_iota(jnp.int32, last.shape, 0) == 0
    two_before, before = [jnp.where(top, 0.0, pltpu.roll(rows, 1, 0)) for rows in (last, end)]
    return [
        (taps[0:1] * now + taps[1:2] * one + taps[2:3] * two).astype(bf16).astype(f32)
        for now, one, two in ((first, before, two_before), (second, first, before))
    ]


def put_first_rows(z, held, products):
    for k, (left, right) in enumerate(products):
        held[pl.ds(k, z.blocks, stride=z.pitch), :] = (left * right).astype(bf16).astype(f32)


def signal_grad_kernel(
    z, data_ref, taps_ref, filter_ref, coarse_ref, fine_ref, inv_ref, back_ref, spec_ref, out_ref, held, parts
):
    load_longer(z, data_ref, held)
    put_first_rows(z, held, zip(first_features(z, held, 0, taps_ref[2]), spare_rows(z, held, 4, 2)))
    coarse_forward(z, held, coarse_ref, parts, False)

    def body(a, carry):
        spec = fine_forward(z, fine_ref, parts, a)
        spec_ref[a] = spec.astype(spec_ref.dtype)
        fine_inverse(z, inv_ref, (parts,), a, (times(spec, filter_ref[a].astype(f32), z.rows, True),))
        return carry

    lax.fori_loop(0, z.half, body, 0, unroll=11)
    coarse_inverse(z, parts, back_ref, held)
    store_blocks(z, held, out_ref)


def conv_out_kernel(
    z,
    data_ref,
    taps_ref,
    filter_ref,
    grad_ref,
    coarse_ref,
    fine_ref,
    inv_ref,
    back_ref,
    out_ref,
    long_ref,
    held,
    parts,
    more,
):
    load_longer(z, data_ref, held)
    put_first_rows(
        z, held, zip(first_features(z, held, 0, taps_ref[0]), first_features(z, held, 4, taps_ref[1]))
    )
    coarse_forward(z, held, coarse_ref, parts, False)
    spare = (z.parts - 2 * z.half) * z.pitch
    if spare:
        more[pl.ds(2 * z.half * z.pitch, spare), :] = jnp.zeros((spare, z.width), f32)

    def body(a, carry):
        spec = fine_forward(z, fine_ref, parts, a)
        conv = times(spec, filter_ref[a].astype(f32), z.rows, False)
        long = times(grad_ref[a].astype(f32), spec, z.rows, True)
        fine_inverse(z, inv_ref, (parts, more), a, (conv, long))
        return carry

    lax.fori_loop(0, z.half, body, 0, unroll=11)
    coarse_inverse(z, parts, back_ref, held)
    store_blocks(z, held, out_ref)
    coarse_inverse(z, more, back_ref, held)

    def done(i, carry):
        long_ref[pl.ds(pl.multiple_of(i * z.rows, 8), z.rows), :] = held[rows_at(z, i), :]
        return carry

    lax.fori_loop(0, z.blocks, done, 0, unroll=4)


def channel_call(z, kernel, operands, outs, name, cost_us, arrays=1):
    whole = pl.BlockSpec(memory_space=pltpu.VMEM)
    return pl.pallas_call(
        kernel,
        out_shape=outs,
        in_specs=[whole] * len(operands),
        out_specs=[whole] * len(outs),
        scratch_shapes=[
            pltpu.VMEM((z.blocks * z.pitch, z.width), f32),
        ]
        + [pltpu.VMEM((z.parts * z.pitch, z.width), f32)] * arrays,
        compiler_params=pltpu.CompilerParams(vmem_limit_bytes=(16 + 7 * arrays) << 20),
        cost_estimate=pl.CostEstimate(flops=0, bytes_accessed=int(cost_us * 3e6), transcendentals=0),
        name=name,
    )(*operands)


def delayed(rows, before, lag):
    moved = pltpu.roll(rows, lag, 0)
    if before is None:
        return moved
    index = lax.broadcasted_iota(jnp.int32, rows.shape, 0)
    for i in range(lag):
        moved = jnp.where(index == i, before[2 - lag + i : 3 - lag + i], moved)
    return moved


def feature(source, halo, which, taps_ref):
    rows = source.astype(f32)
    before = None if halo is None else halo[2 * which : 2 * which + 2]
    one, two = delayed(rows, before, 1), delayed(rows, before, 2)
    taps = taps_ref[which]
    feat = taps[0:1] * rows + taps[1:2] * one + taps[2:3] * two
    return feat.astype(bf16).astype(f32), (rows, one, two)


def outward(out_ref, value):
    for j in range(value.shape[1] // out_ref.shape[2]):
        width = out_ref.shape[2]
        out_ref[j] = value[:, j * width : (j + 1) * width].astype(out_ref.dtype)


def inward(in_ref):
    return jnp.concatenate([in_ref[j] for j in range(in_ref.shape[0])], axis=1).astype(f32)


def outer_kernel(out_ref, cot_ref, taps_ref, outer_ref):
    rows, cot = out_ref[...].astype(f32), cot_ref[...].astype(f32)
    feat_out, _ = feature(out_ref[...], None, 2, taps_ref)
    more = collect([rows[rows.shape[0] - 2 :], rows[0:2], cot[0:2]], PAD, f32)
    outward(outer_ref, jnp.concatenate([feat_out * cot, more], axis=0))


def signal_kernel(gate_ref, value_ref, taps_ref, signal_ref):
    feat_gate, (gate, _, _) = feature(gate_ref[...], None, 0, taps_ref)
    feat_value, (value, _, _) = feature(value_ref[...], None, 1, taps_ref)
    count = gate.shape[0]
    more = collect([gate[count - 2 :], gate[0:2], value[count - 2 :], value[0:2]], PAD, f32)
    outward(signal_ref, jnp.concatenate([feat_gate * feat_value, more], axis=0))


def edges_kernel(gate_ref, value_ref, out_ref, edge_ref):
    rows = [ref[...].astype(f32)[ref.shape[0] - 2 :] for ref in (gate_ref, value_ref, out_ref)]
    edge_ref[...] = collect(rows, 8, bf16)


def adjoint(grad, after, taps):
    index = lax.broadcasted_iota(jnp.int32, grad.shape, 0)
    last = grad.shape[0] - 1
    one = jnp.where(index == last, after[0:1], pltpu.roll(grad, last, 0))
    two = pltpu.roll(grad, last - 1, 0)
    two = jnp.where(index == last - 1, after[0:1], jnp.where(index == last, after[1:2], two))
    return (taps[0:1] * grad + taps[1:2] * one + taps[2:3] * two).astype(bf16)


def collect(pieces, rows, dtype):
    made = jnp.concatenate(pieces, axis=0)
    spare = rows - made.shape[0]
    if spare:
        made = jnp.concatenate([made, jnp.zeros((spare, made.shape[1]), made.dtype)], axis=0)
    return made.astype(dtype)


def lag_sums(grad, lags):
    return [jnp.sum(grad * lag, axis=0, keepdims=True) for lag in lags]


def store_sums(sums_ref, sums):
    made, width = jnp.concatenate(sums, axis=0), sums_ref.shape[2]
    for j in range(sums_ref.shape[0]):
        sums_ref[j] = made[:, j * width : (j + 1) * width]


def input_grads_kernel(
    sig_ref,
    gate_ref,
    value_ref,
    halo_ref,
    taps_ref,
    sums_ref,
    head_ref,
    tail_ref,
    grad_gate_ref,
    grad_value_ref,
):
    halo = halo_ref[...].astype(f32)
    sig = inward(sig_ref)
    feat_gate, gate_lags = feature(gate_ref[...], halo, 0, taps_ref)
    feat_value, value_lags = feature(value_ref[...], halo, 1, taps_ref)
    gate_grad = (sig * feat_value).astype(bf16).astype(f32)
    value_grad = (sig * feat_gate).astype(bf16).astype(f32)
    store_sums(sums_ref, lag_sums(gate_grad, gate_lags) + lag_sums(value_grad, value_lags))
    count = sig.shape[0]
    head_ref[...] = collect([gate_grad[0:2], value_grad[0:2]], 8, bf16)
    tail_ref[...] = collect([gate_grad[count - 2 :], value_grad[count - 2 :]], 8, bf16)
    none = jnp.zeros((2, sig.shape[1]), f32)
    grad_gate_ref[...] = adjoint(gate_grad, none, taps_ref[0])
    grad_value_ref[...] = adjoint(value_grad, none, taps_ref[1])


def finish_kernel(gate_ref, value_ref, next_ref, tail_ref, taps_ref, grad_gate_ref, grad_value_ref):
    head, tail = next_ref[...].astype(f32), tail_ref[...].astype(f32)
    for k, (old_ref, new_ref) in enumerate(((gate_ref, grad_gate_ref), (value_ref, grad_value_ref))):
        taps = taps_ref[k]
        t0, t1 = tail[2 * k : 2 * k + 1], tail[2 * k + 1 : 2 * k + 2]
        h0, h1 = head[2 * k : 2 * k + 1], head[2 * k + 1 : 2 * k + 2]
        old = old_ref[...].astype(f32)
        index = lax.broadcasted_iota(jnp.int32, old.shape, 0)
        last = old.shape[0] - 1
        new = jnp.where(index == last - 1, taps[0:1] * t0 + taps[1:2] * t1 + taps[2:3] * h0, old)
        new = jnp.where(index == last, taps[0:1] * t1 + taps[1:2] * h0 + taps[2:3] * h1, new)
        new_ref[...] = new.astype(bf16)


def output_sums_kernel(conv_ref, out_ref, cot_ref, halo_ref, in_sums_ref, packet_ref, head_ref):
    before = halo_ref[...].astype(f32)[4:6]
    out_grad = (cot_ref[...].astype(f32) * inward(conv_ref)).astype(bf16).astype(f32)
    rows = out_ref[...].astype(f32)
    lags = (rows, delayed(rows, before, 1), delayed(rows, before, 2))
    sums, ins = jnp.concatenate(lag_sums(out_grad, lags), axis=0), in_sums_ref[...]
    head_ref[...] = collect([out_grad[0:2]], 8, bf16)
    count, pack, width = packet_ref.shape
    quarter = sums.shape[1] // 4
    part = quarter // 4
    for n in range(4):
        pieces = [
            sums[:, q * quarter + n * part + h : q * quarter + n * part + h + width]
            for q in range(4)
            for h in range(0, part, width)
        ]
        pieces += [ins[:, n * part + h : n * part + h + width] for h in range(0, part, width)]
        packet = collect(pieces, pack, bf16)
        for depth in range(count // 4):
            packet_ref[(n // 2) * (count // 2) + 2 * depth + n % 2] = packet


def packet_sums_kernel(packet_ref, total_ref):
    count, _, width = packet_ref.shape
    halves = total_ref.shape[0] // 36
    outs = 12 * halves
    packets = [packet_ref[d].astype(f32) for d in range(count)]
    near = [
        functools.reduce(jnp.add, [packets[(q // 2) * (count // 2) + 2 * depth + q % 2] for depth in range(count // 4)])
        for q in range(4)
    ]
    whole = (near[0] + near[1]) + (near[2] + near[3])
    pieces = [whole[:outs]] + [part[outs : outs + 6 * halves] for part in near]
    total_ref[...] = jnp.concatenate(pieces, axis=0)


def short_kernel(me_ref, held_ref, short_ref):
    quarter = short_ref.shape[2] // 4
    part, width = quarter // 4, held_ref.shape[2]
    halves = part // width
    for n in range(4):
        held = held_ref[me_ref[0] ^ n]
        for q in range(4):
            for h in range(halves):
                start = q * quarter + n * part + h * width
                out_row = (q * halves + h) * 3
                in_row = 12 * halves + (q * halves + h) * 6
                short_ref[0, :, start : start + width] = held[in_row : in_row + 3]
                short_ref[1, :, start : start + width] = held[in_row + 3 : in_row + 6]
                short_ref[2, :, start : start + width] = held[out_row : out_row + 3]


def mixed_kernel(conv_ref, out_ref, halo_ref, taps_ref, mixed_ref):
    feat_out, _ = feature(out_ref[...], halo_ref[...].astype(f32), 2, taps_ref)
    mixed_ref[...] = (feat_out * inward(conv_ref)).astype(bf16)


def output_grad_kernel(conv_ref, cot_ref, next_ref, taps_ref, grad_ref):
    out_grad = (cot_ref[...].astype(f32) * inward(conv_ref)).astype(bf16).astype(f32)
    grad_ref[...] = adjoint(out_grad, next_ref[...].astype(f32)[0:2], taps_ref[2])


def position_call(z, kernel, operands, kinds, out_kinds, channels, name, cost_us, tile=TILE, aliases=None, vmem=14):

    quarter = channels // 4

    def spec(kind):
        return {
            "rows": pl.BlockSpec((z.rows, tile), lambda i: (0, i)),
            "moved": pl.BlockSpec((tile // z.width, z.rows, z.width), lambda i: (i, 0, 0)),
            "edge": pl.BlockSpec((8, tile), lambda i: (0, i)),
            "six": pl.BlockSpec((tile // quarter, 6, quarter), lambda i: (i, 0, 0)),
            "near": pl.BlockSpec((6, quarter), lambda i: (0, 0)),
            "taps": pl.BlockSpec((3, 3, tile), lambda i: (0, 0, i)),
            "packet": pl.BlockSpec((z.blocks, z.pack, z.width), lambda i: (0, 0, 0)),
            "longer": pl.BlockSpec((tile // z.width, z.pitch, z.width), lambda i: (i, 0, 0)),
            "last": pl.BlockSpec((16, tile), lambda i: (z.rows // 16 - 1, i)),
        }[kind]

    shapes = {
        "rows": jax.ShapeDtypeStruct((z.rows, channels), bf16),
        "last": jax.ShapeDtypeStruct((z.rows, channels), bf16),
        "moved": jax.ShapeDtypeStruct((channels // z.width, z.rows, z.width), bf16),
        "longer": jax.ShapeDtypeStruct((channels // z.width, z.pitch, z.width), bf16),
        "packet": jax.ShapeDtypeStruct((z.blocks, z.pack, z.width), bf16),
        "edge": jax.ShapeDtypeStruct((8, channels), bf16),
        "six": jax.ShapeDtypeStruct((4, 6, quarter), f32),
    }
    return pl.pallas_call(
        kernel,
        grid=(channels // tile,),
        out_shape=[shapes[k] for k in out_kinds],
        in_specs=[spec(k) for k in kinds],
        out_specs=[spec(k) for k in out_kinds],
        input_output_aliases=aliases or {},
        compiler_params=pltpu.CompilerParams(vmem_limit_bytes=int(vmem * 2**20)),
        cost_estimate=pl.CostEstimate(flops=0, bytes_accessed=int(cost_us * 3e6), transcendentals=0),
        name=name,
    )(*operands)


def small_call(kernel, operands, out, name, scalars=0):
    spaces = [pltpu.SMEM] * scalars + [pltpu.VMEM] * (len(operands) - scalars)
    return pl.pallas_call(
        kernel,
        out_shape=[out],
        in_specs=[pl.BlockSpec(memory_space=space) for space in spaces],
        out_specs=[pl.BlockSpec(memory_space=pltpu.VMEM)],
        compiler_params=pltpu.CompilerParams(vmem_limit_bytes=8 << 20),
        cost_estimate=pl.CostEstimate(flops=0, bytes_accessed=3000000, transcendentals=0),
        name=name,
    )(*operands)


class Near:
    def __init__(self, size):
        self.size, self.offsets = size, (1, size // 2, size // 2 + 1)
        me = lax.axis_index("seq")
        self.quarter = me % 2 + 2 * (me // (size // 2))

    def swap(self, value, bits):
        return lax.ppermute(value, "seq", [(i, i ^ bits) for i in range(self.size)])

    def piece(self, value, which):
        return lax.dynamic_index_in_dim(value, which, 0, keepdims=False)

    def scatter(self, value):
        arrived = [self.swap(self.piece(value, self.quarter ^ (k + 1)), bits) for k, bits in enumerate(self.offsets)]
        return (self.piece(value, self.quarter) + arrived[0]) + (arrived[1] + arrived[2])

    def gather(self, value):
        return jnp.stack([value] + [self.swap(value, bits) for bits in self.offsets])


def exchange(value):
    return lax.all_to_all(value, "seq", split_axis=0, concat_axis=0, tiled=True)


def local(size, gate_in, value_in, gate_out, cotangent, long_filter, short_filters):
    rows, channels = gate_in.shape
    z = Sizes(size, rows, long_filter.shape[1])
    coarse, twice, fine, inv, back = [jnp.asarray(t) for t in tables(z)]
    spec_shape = jax.ShapeDtypeStruct((z.half, 2 * z.rows, z.width), bf16)
    moved_shape = jax.ShapeDtypeStruct((z.blocks, z.rows, z.width), bf16)
    onward = [(i, i + 1) for i in range(size - 1)]
    backward = [(i + 1, i) for i in range(size - 1)]

    def position(kernel, operands, kinds, outs, name, cost_us, **more):
        return position_call(z, kernel, operands, kinds, outs, channels, name, cost_us, **more)

    (outer,) = position(
        outer_kernel,
        (gate_out, cotangent, short_filters),
        ("rows", "rows", "taps"),
        ("longer",),
        "outer",
        4,
        vmem=60,
    )
    outer, last_gate = lax.optimization_barrier((outer, gate_in))
    (edges,) = position(
        edges_kernel, (last_gate, value_in, gate_out), ("last",) * 3, ("edge",), "edges", 1, tile=channels
    )
    halo = lax.ppermute(edges, "seq", onward)
    (signal,) = position(
        signal_kernel, (gate_in, value_in, short_filters), ("rows", "rows", "taps"), ("longer",), "signal", 4
    )
    outer_moved = exchange(outer)
    taps_here = lax.dynamic_slice_in_dim(short_filters, lax.axis_index("seq") * z.width, z.width, 2)
    (filter_spec,) = channel_call(
        z, functools.partial(filter_kernel, z), (long_filter, twice, fine), (spec_shape,), "filter_spec", 8
    )
    signal, filter_spec, halo = lax.optimization_barrier((signal, filter_spec, halo))
    signal_moved = exchange(signal)
    outer_spec, sig_grad = channel_call(
        z,
        functools.partial(signal_grad_kernel, z),
        (outer_moved, taps_here, filter_spec, coarse, fine, inv, back),
        (spec_shape, moved_shape),
        "signal_grad",
        16,
    )
    sig_rows = exchange(sig_grad)
    conv_out, grad_long = channel_call(
        z,
        functools.partial(conv_out_kernel, z),
        (signal_moved, taps_here, filter_spec, outer_spec, coarse, fine, inv, back),
        (moved_shape, jax.ShapeDtypeStruct((z.blocks * z.rows, z.width), f32)),
        "conv_out",
        22,
        arrays=2,
    )
    conv_rows = exchange(conv_out)
    in_sums, in_head, in_tail, grad_gate, grad_value = position(
        input_grads_kernel,
        (sig_rows, gate_in, value_in, halo, short_filters),
        ("moved", "rows", "rows", "edge", "taps"),
        ("six", "edge", "edge", "rows", "rows"),
        "input_grads",
        6,
    )
    near = Near(size)
    in_sums = near.scatter(in_sums)
    in_after = lax.ppermute(in_head, "seq", backward)
    packets, out_head = position(
        output_sums_kernel,
        (conv_rows, gate_out, cotangent, halo, in_sums),
        ("moved", "rows", "rows", "edge", "near"),
        ("packet", "edge"),
        "output_sums",
        3,
        tile=channels,
    )
    after = lax.ppermute(out_head, "seq", backward)
    packets = exchange(packets)
    (mixed,) = position(
        mixed_kernel,
        (conv_rows, gate_out, halo, short_filters),
        ("moved", "rows", "edge", "taps"),
        ("rows",),
        "mixed",
        3,
    )
    (grad_out,) = position(
        output_grad_kernel,
        (conv_rows, cotangent, after, short_filters),
        ("moved", "rows", "edge", "taps"),
        ("rows",),
        "output_grad",
        3,
    )
    grad_gate, grad_value = position(
        finish_kernel,
        (grad_gate, grad_value, in_after, in_tail, short_filters),
        ("last", "last", "edge", "edge", "taps"),
        ("last", "last"),
        "finish_input_grads",
        2,
        tile=channels,
        aliases={0: 0, 1: 1},
    )
    packets, mixed, grad_out, grad_gate, grad_value = lax.optimization_barrier(
        (packets, mixed, grad_out, grad_gate, grad_value)
    )
    (total,) = small_call(
        packet_sums_kernel, (packets,), jax.ShapeDtypeStruct((36 * z.halves, z.width), f32), "packet_sums"
    )
    held = near.gather(total)
    quarter = near.quarter.astype(jnp.int32).reshape(1)
    (grad_short,) = small_call(
        short_kernel, (quarter, held), jax.ShapeDtypeStruct((3, 3, channels), f32), "grad_short", scalars=1
    )
    return (mixed, grad_gate, grad_value, grad_out, grad_long, grad_short)


def solution(mesh):
    spread = P(("grp", "seq"), None)
    return jax.shard_map(
        functools.partial(local, mesh.shape["seq"]),
        mesh=mesh,
        in_specs=(spread, spread, spread, spread, P(None, "seq"), P()),
        out_specs=(spread, spread, spread, spread, P("grp", "seq"), P("grp", None, None)),
        check_vma=False,
    )
```

```python
import functools

import jax
import jax.numpy as jnp
import ml_dtypes
import numpy as np
from jax import lax
from jax.experimental import pallas as pl
from jax.experimental.pallas import tpu as pltpu
from jax.sharding import PartitionSpec as P

bf16 = jnp.bfloat16
f32 = jnp.float32

TILE = 2048
GROUP = 32
PAD = 8


class Sizes:
    def __init__(self, blocks, rows, width):
        self.blocks, self.rows, self.width = blocks, rows, width
        self.half = blocks + 1
        self.parts = -(-2 * self.half // 8) * 8
        self.pitch = rows + PAD
        self.length = 2 * blocks * rows
        self.halves = blocks // 16
        self.pack = -(-18 * self.halves // 8) * 8


def tables(z):
    a, b = np.arange(z.half), np.arange(z.blocks)
    turn = 2 * np.pi * ((a[:, None] * b[None, :]) % (2 * z.blocks)) / (2 * z.blocks)
    coarse = np.zeros((z.parts, z.blocks))
    coarse[0 : 2 * z.half : 2] = np.cos(turn)
    coarse[1 : 2 * z.half : 2] = -np.sin(turn)
    weight = np.where((a == 0) | (a == z.blocks), 1.0, 2.0) / z.length
    back = np.zeros((z.blocks, z.parts))
    back[:, 0 : 2 * z.half : 2] = (np.cos(turn) * weight[:, None]).T
    back[:, 1 : 2 * z.half : 2] = (-np.sin(turn) * weight[:, None]).T
    r = np.arange(z.rows)
    phase = ((a[:, None, None] + 2 * z.blocks * r[None, :, None]) * r[None, None, :]) % z.length
    cos_w, sin_w = np.cos(2 * np.pi * phase / z.length), np.sin(2 * np.pi * phase / z.length)
    fine = np.concatenate([np.concatenate([cos_w, sin_w], 2), np.concatenate([-sin_w, cos_w], 2)], 1)
    twice = np.concatenate([coarse, coarse], 1)
    return [t.astype(ml_dtypes.bfloat16) for t in (coarse, twice, fine, fine.transpose(0, 2, 1), back)]


def rows_at(z, block):
    return pl.ds(pl.multiple_of(block * z.pitch, 8), z.rows)


def coarse_forward(z, held, coarse_ref, parts, split):
    coarse = coarse_ref[...]

    def body(step, carry):
        columns = []
        for j in range(GROUP):
            value = held[pl.ds(step * GROUP + j, z.blocks, stride=z.pitch), :]
            high = value.astype(bf16)
            if split:
                high = jnp.concatenate([high, (value - high.astype(f32)).astype(bf16)], axis=0)
            columns.append(high)
        out = jnp.dot(coarse, jnp.concatenate(columns, axis=1), preferred_element_type=f32)
        for j in range(GROUP):
            parts[pl.ds(step * GROUP + j, z.parts, stride=z.pitch), :] = out[:, j * z.width : (j + 1) * z.width]
        return carry

    lax.fori_loop(0, z.rows // GROUP, body, 0)


def coarse_inverse(z, parts, back_ref, held):
    back = back_ref[...]

    def body(step, carry):
        columns = [parts[pl.ds(step * GROUP + j, z.parts, stride=z.pitch), :].astype(bf16) for j in range(GROUP)]
        out = jnp.dot(back, jnp.concatenate(columns, axis=1), preferred_element_type=f32)
        for j in range(GROUP):
            held[pl.ds(step * GROUP + j, z.blocks, stride=z.pitch), :] = out[:, j * z.width : (j + 1) * z.width]
        return carry

    lax.fori_loop(0, z.rows // GROUP, body, 0)


def fine_forward(z, fine_ref, parts, a):
    re = parts[rows_at(z, 2 * a), :].astype(bf16)
    im = parts[rows_at(z, 2 * a + 1), :].astype(bf16)
    return jnp.dot(fine_ref[a], jnp.concatenate([re, im], axis=0), preferred_element_type=f32)


def fine_inverse(z, fine_ref, targets, a, pairs):
    specs = [jnp.concatenate([re.astype(bf16), im.astype(bf16)], axis=0) for re, im in pairs]
    out = jnp.dot(fine_ref[a], jnp.concatenate(specs, axis=1), preferred_element_type=f32)
    for j, parts in enumerate(targets):
        parts[rows_at(z, 2 * a), :] = out[: z.rows, j * z.width : (j + 1) * z.width]
        parts[rows_at(z, 2 * a + 1), :] = out[z.rows :, j * z.width : (j + 1) * z.width]


def load_blocks(z, block_of, held):
    def body(i, carry):
        held[rows_at(z, i), :] = block_of(i).astype(f32)
        return carry

    lax.fori_loop(0, z.blocks, body, 0, unroll=4)


def store_blocks(z, held, out_ref):
    def body(i, carry):
        out_ref[i] = held[rows_at(z, i), :].astype(out_ref.dtype)
        return carry

    lax.fori_loop(0, z.blocks, body, 0, unroll=4)


def filter_kernel(z, filter_ref, twice_ref, fine_ref, spec_ref, held, parts):
    load_blocks(z, lambda i: filter_ref[pl.ds(pl.multiple_of(i * z.rows, 8), z.rows), :], held)
    coarse_forward(z, held, twice_ref, parts, True)

    def body(a, carry):
        spec_ref[a] = fine_forward(z, fine_ref, parts, a).astype(spec_ref.dtype)
        return carry

    lax.fori_loop(0, z.half, body, 0, unroll=11)


def times(spec, other, rows, conj):
    s_re, s_im, h_re, h_im = spec[:rows], spec[rows:], other[:rows], other[rows:]
    if conj:
        return s_re * h_re + s_im * h_im, s_im * h_re - s_re * h_im
    return s_re * h_re - s_im * h_im, s_re * h_im + s_im * h_re


def load_longer(z, data_ref, held):
    def body(i, carry):
        held[pl.ds(pl.multiple_of(i * z.pitch, 8), z.pitch), :] = data_ref[i].astype(f32)
        return carry

    lax.fori_loop(0, z.blocks, body, 0, unroll=4)


def spare_rows(z, held, start, count):
    return [held[pl.ds(z.rows + start + k, z.blocks, stride=z.pitch), :] for k in range(count)]


def first_features(z, held, start, taps):
    last, end, first, second = spare_rows(z, held, start, 4)
    top = lax.broadcasted_iota(jnp.int32, last.shape, 0) == 0
    two_before, before = [jnp.where(top, 0.0, pltpu.roll(rows, 1, 0)) for rows in (last, end)]
    return [
        (taps[0:1] * now + taps[1:2] * one + taps[2:3] * two).astype(bf16).astype(f32)
        for now, one, two in ((first, before, two_before), (second, first, before))
    ]


def put_first_rows(z, held, products):
    for k, (left, right) in enumerate(products):
        held[pl.ds(k, z.blocks, stride=z.pitch), :] = (left * right).astype(bf16).astype(f32)


def signal_grad_kernel(
    z, data_ref, taps_ref, filter_ref, coarse_ref, fine_ref, inv_ref, back_ref, spec_ref, out_ref, held, parts
):
    load_longer(z, data_ref, held)
    put_first_rows(z, held, zip(first_features(z, held, 0, taps_ref[2]), spare_rows(z, held, 4, 2)))
    coarse_forward(z, held, coarse_ref, parts, False)

    def body(a, carry):
        spec = fine_forward(z, fine_ref, parts, a)
        spec_ref[a] = spec.astype(spec_ref.dtype)
        fine_inverse(z, inv_ref, (parts,), a, (times(spec, filter_ref[a].astype(f32), z.rows, True),))
        return carry

    lax.fori_loop(0, z.half, body, 0, unroll=11)
    coarse_inverse(z, parts, back_ref, held)
    store_blocks(z, held, out_ref)


def conv_out_kernel(
    z,
    data_ref,
    taps_ref,
    filter_ref,
    grad_ref,
    coarse_ref,
    fine_ref,
    inv_ref,
    back_ref,
    out_ref,
    long_ref,
    held,
    parts,
    more,
):
    load_longer(z, data_ref, held)
    put_first_rows(
        z, held, zip(first_features(z, held, 0, taps_ref[0]), first_features(z, held, 4, taps_ref[1]))
    )
    coarse_forward(z, held, coarse_ref, parts, False)
    spare = (z.parts - 2 * z.half) * z.pitch
    if spare:
        more[pl.ds(2 * z.half * z.pitch, spare), :] = jnp.zeros((spare, z.width), f32)

    def body(a, carry):
        spec = fine_forward(z, fine_ref, parts, a)
        conv = times(spec, filter_ref[a].astype(f32), z.rows, False)
        long = times(grad_ref[a].astype(f32), spec, z.rows, True)
        fine_inverse(z, inv_ref, (parts, more), a, (conv, long))
        return carry

    lax.fori_loop(0, z.half, body, 0, unroll=11)
    coarse_inverse(z, parts, back_ref, held)
    store_blocks(z, held, out_ref)
    coarse_inverse(z, more, back_ref, held)

    def done(i, carry):
        long_ref[pl.ds(pl.multiple_of(i * z.rows, 8), z.rows), :] = held[rows_at(z, i), :]
        return carry

    lax.fori_loop(0, z.blocks, done, 0, unroll=4)


def channel_call(z, kernel, operands, outs, name, cost_us, arrays=1):
    whole = pl.BlockSpec(memory_space=pltpu.VMEM)
    return pl.pallas_call(
        kernel,
        out_shape=outs,
        in_specs=[whole] * len(operands),
        out_specs=[whole] * len(outs),
        scratch_shapes=[
            pltpu.VMEM((z.blocks * z.pitch, z.width), f32),
        ]
        + [pltpu.VMEM((z.parts * z.pitch, z.width), f32)] * arrays,
        compiler_params=pltpu.CompilerParams(vmem_limit_bytes=(16 + 7 * arrays) << 20),
        cost_estimate=pl.CostEstimate(flops=0, bytes_accessed=int(cost_us * 3e6), transcendentals=0),
        name=name,
    )(*operands)


def delayed(rows, before, lag):
    moved = pltpu.roll(rows, lag, 0)
    if before is None:
        return moved
    index = lax.broadcasted_iota(jnp.int32, rows.shape, 0)
    for i in range(lag):
        moved = jnp.where(index == i, before[2 - lag + i : 3 - lag + i], moved)
    return moved


def feature(source, halo, which, taps_ref):
    rows = source.astype(f32)
    before = None if halo is None else halo[2 * which : 2 * which + 2]
    one, two = delayed(rows, before, 1), delayed(rows, before, 2)
    taps = taps_ref[which]
    feat = taps[0:1] * rows + taps[1:2] * one + taps[2:3] * two
    return feat.astype(bf16).astype(f32), (rows, one, two)


def outward(out_ref, value):
    for j in range(value.shape[1] // out_ref.shape[2]):
        width = out_ref.shape[2]
        out_ref[j] = value[:, j * width : (j + 1) * width].astype(out_ref.dtype)


def inward(in_ref):
    return jnp.concatenate([in_ref[j] for j in range(in_ref.shape[0])], axis=1).astype(f32)


def outer_kernel(out_ref, cot_ref, taps_ref, outer_ref):
    rows, cot = out_ref[...].astype(f32), cot_ref[...].astype(f32)
    feat_out, _ = feature(out_ref[...], None, 2, taps_ref)
    more = collect([rows[rows.shape[0] - 2 :], rows[0:2], cot[0:2]], PAD, f32)
    outward(outer_ref, jnp.concatenate([feat_out * cot, more], axis=0))


def signal_kernel(gate_ref, value_ref, taps_ref, signal_ref):
    feat_gate, (gate, _, _) = feature(gate_ref[...], None, 0, taps_ref)
    feat_value, (value, _, _) = feature(value_ref[...], None, 1, taps_ref)
    count = gate.shape[0]
    more = collect([gate[count - 2 :], gate[0:2], value[count - 2 :], value[0:2]], PAD, f32)
    outward(signal_ref, jnp.concatenate([feat_gate * feat_value, more], axis=0))


def edges_kernel(gate_ref, value_ref, out_ref, edge_ref):
    rows = [ref[...].astype(f32)[ref.shape[0] - 2 :] for ref in (gate_ref, value_ref, out_ref)]
    edge_ref[...] = collect(rows, 8, bf16)


def adjoint(grad, after, taps):
    index = lax.broadcasted_iota(jnp.int32, grad.shape, 0)
    last = grad.shape[0] - 1
    one = jnp.where(index == last, after[0:1], pltpu.roll(grad, last, 0))
    two = pltpu.roll(grad, last - 1, 0)
    two = jnp.where(index == last - 1, after[0:1], jnp.where(index == last, after[1:2], two))
    return (taps[0:1] * grad + taps[1:2] * one + taps[2:3] * two).astype(bf16)


def collect(pieces, rows, dtype):
    made = jnp.concatenate(pieces, axis=0)
    spare = rows - made.shape[0]
    if spare:
        made = jnp.concatenate([made, jnp.zeros((spare, made.shape[1]), made.dtype)], axis=0)
    return made.astype(dtype)


def lag_sums(grad, lags):
    return [jnp.sum(grad * lag, axis=0, keepdims=True) for lag in lags]


def store_sums(sums_ref, sums):
    made, width = jnp.concatenate(sums, axis=0), sums_ref.shape[2]
    for j in range(sums_ref.shape[0]):
        sums_ref[j] = made[:, j * width : (j + 1) * width]


def input_grads_kernel(
    sig_ref,
    gate_ref,
    value_ref,
    halo_ref,
    taps_ref,
    sums_ref,
    head_ref,
    tail_ref,
    grad_gate_ref,
    grad_value_ref,
):
    halo = halo_ref[...].astype(f32)
    sig = inward(sig_ref)
    feat_gate, gate_lags = feature(gate_ref[...], halo, 0, taps_ref)
    feat_value, value_lags = feature(value_ref[...], halo, 1, taps_ref)
    gate_grad = (sig * feat_value).astype(bf16).astype(f32)
    value_grad = (sig * feat_gate).astype(bf16).astype(f32)
    store_sums(sums_ref, lag_sums(gate_grad, gate_lags) + lag_sums(value_grad, value_lags))
    count = sig.shape[0]
    head_ref[...] = collect([gate_grad[0:2], value_grad[0:2]], 8, bf16)
    tail_ref[...] = collect([gate_grad[count - 2 :], value_grad[count - 2 :]], 8, bf16)
    none = jnp.zeros((2, sig.shape[1]), f32)
    grad_gate_ref[...] = adjoint(gate_grad, none, taps_ref[0])
    grad_value_ref[...] = adjoint(value_grad, none, taps_ref[1])


def finish_kernel(gate_ref, value_ref, next_ref, tail_ref, taps_ref, grad_gate_ref, grad_value_ref):
    head, tail = next_ref[...].astype(f32), tail_ref[...].astype(f32)
    for k, (old_ref, new_ref) in enumerate(((gate_ref, grad_gate_ref), (value_ref, grad_value_ref))):
        taps = taps_ref[k]
        t0, t1 = tail[2 * k : 2 * k + 1], tail[2 * k + 1 : 2 * k + 2]
        h0, h1 = head[2 * k : 2 * k + 1], head[2 * k + 1 : 2 * k + 2]
        old = old_ref[...].astype(f32)
        index = lax.broadcasted_iota(jnp.int32, old.shape, 0)
        last = old.shape[0] - 1
        new = jnp.where(index == last - 1, taps[0:1] * t0 + taps[1:2] * t1 + taps[2:3] * h0, old)
        new = jnp.where(index == last, taps[0:1] * t1 + taps[1:2] * h0 + taps[2:3] * h1, new)
        new_ref[...] = new.astype(bf16)


def output_sums_kernel(conv_ref, out_ref, cot_ref, halo_ref, in_sums_ref, packet_ref):
    before = halo_ref[...].astype(f32)[4:6]
    out_grad = (cot_ref[...].astype(f32) * inward(conv_ref)).astype(bf16).astype(f32)
    rows = out_ref[...].astype(f32)
    lags = (rows, delayed(rows, before, 1), delayed(rows, before, 2))
    sums, ins = jnp.concatenate(lag_sums(out_grad, lags), axis=0), in_sums_ref[...]
    count, pack, width = packet_ref.shape
    quarter = sums.shape[1] // 4
    part = quarter // 4
    for n in range(4):
        pieces = [
            sums[:, q * quarter + n * part + h : q * quarter + n * part + h + width]
            for q in range(4)
            for h in range(0, part, width)
        ]
        pieces += [ins[:, n * part + h : n * part + h + width] for h in range(0, part, width)]
        packet = collect(pieces, pack, bf16)
        for depth in range(count // 4):
            packet_ref[(n // 2) * (count // 2) + 2 * depth + n % 2] = packet


def packet_sums_kernel(packet_ref, total_ref):
    count, _, width = packet_ref.shape
    halves = total_ref.shape[0] // 36
    outs = 12 * halves
    packets = [packet_ref[d].astype(f32) for d in range(count)]
    near = [
        functools.reduce(jnp.add, [packets[(q // 2) * (count // 2) + 2 * depth + q % 2] for depth in range(count // 4)])
        for q in range(4)
    ]
    whole = (near[0] + near[1]) + (near[2] + near[3])
    pieces = [whole[:outs]] + [part[outs : outs + 6 * halves] for part in near]
    total_ref[...] = jnp.concatenate(pieces, axis=0)


def short_kernel(me_ref, held_ref, short_ref):
    quarter = short_ref.shape[2] // 4
    part, width = quarter // 4, held_ref.shape[2]
    halves = part // width
    for n in range(4):
        held = held_ref[me_ref[0] ^ n]
        for q in range(4):
            for h in range(halves):
                start = q * quarter + n * part + h * width
                out_row = (q * halves + h) * 3
                in_row = 12 * halves + (q * halves + h) * 6
                short_ref[0, :, start : start + width] = held[in_row : in_row + 3]
                short_ref[1, :, start : start + width] = held[in_row + 3 : in_row + 6]
                short_ref[2, :, start : start + width] = held[out_row : out_row + 3]


def mixed_kernel(conv_ref, out_ref, cot_first, halo_ref, taps_ref, mixed_ref, head_ref):
    feat_out, _ = feature(out_ref[...], halo_ref[...].astype(f32), 2, taps_ref)
    conv = inward(conv_ref)
    mixed_ref[...] = (feat_out * conv).astype(bf16)
    head_ref[...] = collect([cot_first[...].astype(f32)[0:2] * conv[0:2]], 8, bf16)


def output_grad_kernel(conv_ref, cot_ref, next_ref, taps_ref, grad_ref):
    out_grad = (cot_ref[...].astype(f32) * inward(conv_ref)).astype(bf16).astype(f32)
    grad_ref[...] = adjoint(out_grad, next_ref[...].astype(f32)[0:2], taps_ref[2])


def position_call(z, kernel, operands, kinds, out_kinds, channels, name, cost_us, tile=TILE, aliases=None, vmem=14):

    quarter = channels // 4

    def spec(kind):
        return {
            "rows": pl.BlockSpec((z.rows, tile), lambda i: (0, i)),
            "moved": pl.BlockSpec((tile // z.width, z.rows, z.width), lambda i: (i, 0, 0)),
            "edge": pl.BlockSpec((8, tile), lambda i: (0, i)),
            "six": pl.BlockSpec((tile // quarter, 6, quarter), lambda i: (i, 0, 0)),
            "near": pl.BlockSpec((6, quarter), lambda i: (0, 0)),
            "taps": pl.BlockSpec((3, 3, tile), lambda i: (0, 0, i)),
            "packet": pl.BlockSpec((z.blocks, z.pack, z.width), lambda i: (0, 0, 0)),
            "longer": pl.BlockSpec((tile // z.width, z.pitch, z.width), lambda i: (i, 0, 0)),
            "first": pl.BlockSpec((16, tile), lambda i: (0, i)),
            "last": pl.BlockSpec((16, tile), lambda i: (z.rows // 16 - 1, i)),
        }[kind]

    shapes = {
        "rows": jax.ShapeDtypeStruct((z.rows, channels), bf16),
        "last": jax.ShapeDtypeStruct((z.rows, channels), bf16),
        "moved": jax.ShapeDtypeStruct((channels // z.width, z.rows, z.width), bf16),
        "longer": jax.ShapeDtypeStruct((channels // z.width, z.pitch, z.width), bf16),
        "packet": jax.ShapeDtypeStruct((z.blocks, z.pack, z.width), bf16),
        "edge": jax.ShapeDtypeStruct((8, channels), bf16),
        "six": jax.ShapeDtypeStruct((4, 6, quarter), f32),
    }
    return pl.pallas_call(
        kernel,
        grid=(channels // tile,),
        out_shape=[shapes[k] for k in out_kinds],
        in_specs=[spec(k) for k in kinds],
        out_specs=[spec(k) for k in out_kinds],
        input_output_aliases=aliases or {},
        compiler_params=pltpu.CompilerParams(vmem_limit_bytes=int(vmem * 2**20)),
        cost_estimate=pl.CostEstimate(flops=0, bytes_accessed=int(cost_us * 3e6), transcendentals=0),
        name=name,
    )(*operands)


def small_call(kernel, operands, out, name, scalars=0):
    spaces = [pltpu.SMEM] * scalars + [pltpu.VMEM] * (len(operands) - scalars)
    return pl.pallas_call(
        kernel,
        out_shape=[out],
        in_specs=[pl.BlockSpec(memory_space=space) for space in spaces],
        out_specs=[pl.BlockSpec(memory_space=pltpu.VMEM)],
        compiler_params=pltpu.CompilerParams(vmem_limit_bytes=8 << 20),
        cost_estimate=pl.CostEstimate(flops=0, bytes_accessed=3000000, transcendentals=0),
        name=name,
    )(*operands)


class Near:
    def __init__(self, size):
        self.size, self.offsets = size, (1, size // 2, size // 2 + 1)
        me = lax.axis_index("seq")
        self.quarter = me % 2 + 2 * (me // (size // 2))

    def swap(self, value, bits):
        return lax.ppermute(value, "seq", [(i, i ^ bits) for i in range(self.size)])

    def piece(self, value, which):
        return lax.dynamic_index_in_dim(value, which, 0, keepdims=False)

    def scatter(self, value):
        arrived = [self.swap(self.piece(value, self.quarter ^ (k + 1)), bits) for k, bits in enumerate(self.offsets)]
        return (self.piece(value, self.quarter) + arrived[0]) + (arrived[1] + arrived[2])

    def gather(self, value):
        return jnp.stack([value] + [self.swap(value, bits) for bits in self.offsets])


def exchange(value):
    return lax.all_to_all(value, "seq", split_axis=0, concat_axis=0, tiled=True)


def local(size, gate_in, value_in, gate_out, cotangent, long_filter, short_filters):
    rows, channels = gate_in.shape
    z = Sizes(size, rows, long_filter.shape[1])
    coarse, twice, fine, inv, back = [jnp.asarray(t) for t in tables(z)]
    spec_shape = jax.ShapeDtypeStruct((z.half, 2 * z.rows, z.width), bf16)
    moved_shape = jax.ShapeDtypeStruct((z.blocks, z.rows, z.width), bf16)
    onward = [(i, i + 1) for i in range(size - 1)]
    backward = [(i + 1, i) for i in range(size - 1)]

    def position(kernel, operands, kinds, outs, name, cost_us, **more):
        return position_call(z, kernel, operands, kinds, outs, channels, name, cost_us, **more)

    (outer,) = position(
        outer_kernel,
        (gate_out, cotangent, short_filters),
        ("rows", "rows", "taps"),
        ("longer",),
        "outer",
        4,
        vmem=60,
    )
    outer, last_gate = lax.optimization_barrier((outer, gate_in))
    (edges,) = position(
        edges_kernel, (last_gate, value_in, gate_out), ("last",) * 3, ("edge",), "edges", 1, tile=channels
    )
    halo = lax.ppermute(edges, "seq", onward)
    (signal,) = position(
        signal_kernel, (gate_in, value_in, short_filters), ("rows", "rows", "taps"), ("longer",), "signal", 4
    )
    outer_moved = exchange(outer)
    taps_here = lax.dynamic_slice_in_dim(short_filters, lax.axis_index("seq") * z.width, z.width, 2)
    (filter_spec,) = channel_call(
        z, functools.partial(filter_kernel, z), (long_filter, twice, fine), (spec_shape,), "filter_spec", 8
    )
    signal, filter_spec, halo = lax.optimization_barrier((signal, filter_spec, halo))
    signal_moved = exchange(signal)
    outer_spec, sig_grad = channel_call(
        z,
        functools.partial(signal_grad_kernel, z),
        (outer_moved, taps_here, filter_spec, coarse, fine, inv, back),
        (spec_shape, moved_shape),
        "signal_grad",
        16,
    )
    sig_rows = exchange(sig_grad)
    conv_out, grad_long = channel_call(
        z,
        functools.partial(conv_out_kernel, z),
        (signal_moved, taps_here, filter_spec, outer_spec, coarse, fine, inv, back),
        (moved_shape, jax.ShapeDtypeStruct((z.blocks * z.rows, z.width), f32)),
        "conv_out",
        22,
        arrays=2,
    )
    conv_rows = exchange(conv_out)
    in_sums, in_head, in_tail, grad_gate, grad_value = position(
        input_grads_kernel,
        (sig_rows, gate_in, value_in, halo, short_filters),
        ("moved", "rows", "rows", "edge", "taps"),
        ("six", "edge", "edge", "rows", "rows"),
        "input_grads",
        6,
    )
    near = Near(size)
    in_sums = near.scatter(in_sums)
    in_after = lax.ppermute(in_head, "seq", backward)
    (packets,) = position(
        output_sums_kernel,
        (conv_rows, gate_out, cotangent, halo, in_sums),
        ("moved", "rows", "rows", "edge", "near"),
        ("packet",),
        "output_sums",
        3,
        tile=channels,
    )
    packets = exchange(packets)
    mixed, out_head = position(
        mixed_kernel,
        (conv_rows, gate_out, cotangent, halo, short_filters),
        ("moved", "rows", "first", "edge", "taps"),
        ("rows", "edge"),
        "mixed",
        3,
    )
    after = lax.ppermute(out_head, "seq", backward)
    (grad_out,) = position(
        output_grad_kernel,
        (conv_rows, cotangent, after, short_filters),
        ("moved", "rows", "edge", "taps"),
        ("rows",),
        "output_grad",
        3,
    )
    grad_gate, grad_value = position(
        finish_kernel,
        (grad_gate, grad_value, in_after, in_tail, short_filters),
        ("last", "last", "edge", "edge", "taps"),
        ("last", "last"),
        "finish_input_grads",
        2,
        tile=channels,
        aliases={0: 0, 1: 1},
    )
    packets, mixed, grad_out, grad_gate, grad_value = lax.optimization_barrier(
        (packets, mixed, grad_out, grad_gate, grad_value)
    )
    (total,) = small_call(
        packet_sums_kernel, (packets,), jax.ShapeDtypeStruct((36 * z.halves, z.width), f32), "packet_sums"
    )
    held = near.gather(total)
    quarter = near.quarter.astype(jnp.int32).reshape(1)
    (grad_short,) = small_call(
        short_kernel, (quarter, held), jax.ShapeDtypeStruct((3, 3, channels), f32), "grad_short", scalars=1
    )
    return (mixed, grad_gate, grad_value, grad_out, grad_long, grad_short)


def solution(mesh):
    spread = P(("grp", "seq"), None)
    return jax.shard_map(
        functools.partial(local, mesh.shape["seq"]),
        mesh=mesh,
        in_specs=(spread, spread, spread, spread, P(None, "seq"), P()),
        out_specs=(spread, spread, spread, spread, P("grp", "seq"), P("grp", None, None)),
        check_vma=False,
    )
```
